32 devices in a mesh: grp: 2 (over y), node: 4 (over z), head: 4 (over x, core).
Axes of the slice: x: 2, y: 2, z: 4, core: 2. Of those that a mesh axis runs over, the one named last changes fastest.
Arguments:
- queries: bfloat16 [2048, 1024], P(('grp', 'node', 'head')), parts along dimension 0, may hold values from -8 to 8
- key_rows: bfloat16 [2048, 1024], P(('grp', 'node', 'head')), parts along dimension 0, may hold values from -8 to 8
- value_rows: bfloat16 [2048, 1024], P(('grp', 'node', 'head')), parts along dimension 0, may hold values from -6 to 6
- out_grads: bfloat16 [2048, 1024], P(('grp', 'node', 'head')), parts along dimension 0, may hold values from -6 to 6
- neighbours: int32 [16, 8], P('grp'), parts along dimension 0, may hold values from 0 to 7, as said below
Outputs:
- attended: bfloat16 [2048, 1024], P(('grp', 'node', 'head')), parts along dimension 0
- query_grad: bfloat16 [2048, 1024], P(('grp', 'node', 'head')), parts along dimension 0
- key_grad: bfloat16 [2048, 1024], P(('grp', 'node', 'head')), parts along dimension 0
- value_grad: bfloat16 [2048, 1024], P(('grp', 'node', 'head')), parts along dimension 0
The draws below stay inside these ranges and needn't reach their ends.
There are 2 independent parts, one for each index of `grp`. The reference program is written for one: setup_inputs(seed, part) draws one part's arguments, and reference() takes and returns one part's arrays. A program takes and returns all parts, laid end to end along the dimension named above; each array names one. Nothing has to cross between parts.
Inputs may be any that keep to these rules, and one draw needn't show every extreme that they name: `neighbours`: the owner of patch p is p // 2. Every listed neighbour of a patch has an owner at distance at most 1 from the patch's owner. The patches of one owner together list exactly 1 distinct patches of each other owner within distance 1 that exists, and none of any other owner.
All inputs are finite; a program needn't handle non-finite values.
Results may differ from the reference program's by a relative error of at most 0.012.
Values may be sent and summed in bfloat16 or wider, within the bound.
No kernel may reach another device: no remote copies, remote signals or barrier semaphores. Data moves between devices by JAX's collectives and lax.ppermute only.
A program may use at most 64 MiB of HBM per device.

```python
import math
import jax
import jax.numpy as jnp
from jax import lax

HEADS = 16
HEAD_DIM = 64
PATCH = 128
NBRS = 8
RADIUS = 1
CAP = 1
PATCH_DEV = 2
D = 1024
PATCHES = 8
NODES = 1024


def draw_queries(key, part):
    inner = jax.random.fold_in(key, 1)
    field = jnp.clip(jax.random.normal(inner, (PATCHES, PATCH, HEADS, HEAD_DIM)), -6.0, 6.0)
    return field.reshape(NODES, D).astype(jnp.bfloat16)


def draw_key_rows(key, part):
    inner = jax.random.fold_in(key, 2)
    field = jnp.clip(jax.random.normal(inner, (PATCHES, PATCH, HEADS, HEAD_DIM)), -6.0, 6.0)
    return field.reshape(NODES, D).astype(jnp.bfloat16)


def draw_neighbours(key, part):
    owners = PATCHES // PATCH_DEV
    inner = jax.random.fold_in(key, 3)
    key_rank, key_turn, key_near = jax.random.split(inner, 3)
    directions = 2 * RADIUS
    offsets = jnp.array(list(range(-RADIUS, 0)) + list(range(1, RADIUS + 1)), jnp.int32)
    rank_keys = jax.random.randint(key_rank, (owners, directions, PATCH_DEV), 0, 1 << 20) * PATCH_DEV + jnp.arange(PATCH_DEV, dtype=jnp.int32)
    ordering = jnp.argsort(rank_keys, axis=-1).astype(jnp.int32)
    rotate = jax.random.randint(key_turn, (owners, directions, 1), 0, CAP)
    picked = (jnp.arange(PATCH_DEV, dtype=jnp.int32)[None, None, :] + rotate) % CAP
    chosen = jnp.take_along_axis(ordering, picked, axis=-1)
    target = jnp.arange(owners, dtype=jnp.int32)[:, None] + offsets[None, :]
    inside_mesh = (target >= 0) & (target < owners)
    remote = jnp.transpose(target[:, :, None] * PATCH_DEV + chosen, (0, 2, 1))
    inside_mesh = jnp.broadcast_to(inside_mesh[:, None, :], remote.shape)
    nearby = jax.random.randint(key_near, (owners, PATCH_DEV, NBRS), 0, PATCH_DEV) + jnp.arange(owners, dtype=jnp.int32)[:, None, None] * PATCH_DEV
    leading = jnp.where(inside_mesh, remote, nearby[:, :, :directions])
    return jnp.concatenate([leading, nearby[:, :, directions:]], -1).reshape(PATCHES, NBRS).astype(jnp.int32)


def shard_levels(stream_key, shape, pieces, smallest, largest):
    level = 1.0
    for axis_at, blocks in pieces:
        steps = jax.random.uniform(jax.random.fold_in(jax.random.fold_in(stream_key, 6), axis_at), (blocks,), jnp.float32, smallest / len(pieces), largest / len(pieces))
        level = level * jnp.repeat(jnp.exp(steps), shape[axis_at] // blocks).reshape((-1,) + (1,) * (len(shape) - 1 - axis_at))
    return level


def bell_draw(stream_key, shape, deviation, bound, shards=(), kind=jnp.bfloat16):
    values = deviation * jax.random.normal(stream_key, shape, jnp.float32)
    if shards:
        values = values * shard_levels(stream_key, shape, shards, -0.22, 0.18)
    return jnp.clip(values, -bound, bound).astype(kind)


def setup_inputs(seed: int = 0, part: int = 0) -> dict:
    keys = jax.random.split(jax.random.key(seed), 6)
    part_splits = jax.random.split(jax.random.fold_in(keys[5], part), 6)
    return {
        "queries": draw_queries(jax.random.fold_in(jax.random.fold_in(keys[5], part), 71), part),
        "key_rows": draw_key_rows(jax.random.fold_in(jax.random.fold_in(keys[5], part), 71), part),
        "value_rows": bell_draw(part_splits[2], (NODES, D), 1.0, 6.0, ((0, 16),)),
        "out_grads": bell_draw(part_splits[3], (NODES, D), 1.0, 6.0, ((0, 16),)),
        "neighbours": draw_neighbours(jax.random.fold_in(jax.random.fold_in(keys[5], part), 71), part),
    }


def to_low(values_in):
    return lax.optimization_barrier(values_in.astype(jnp.bfloat16)).astype(jnp.float32)


def attend_block(query_blk, grad_blk, key_blk, value_blk):
    score_scale = HEAD_DIM ** -0.5
    query_f = query_blk.astype(jnp.float32)
    grad_f = grad_blk.astype(jnp.float32)
    key_f = key_blk.astype(jnp.float32)
    value_f = value_blk.astype(jnp.float32)
    scores = jnp.einsum("bqhd,bkhd->bhqk", query_f, key_f) * score_scale
    row_max = jnp.max(scores, -1, keepdims=True)
    exp_scores = jnp.exp(scores - row_max)
    weights = exp_scores / jnp.sum(exp_scores, -1, keepdims=True)
    weights_low = to_low(weights)
    mixed = jnp.einsum("bhqk,bkhd->bqhd", weights_low, value_f)
    grad_weights = jnp.einsum("bqhd,bkhd->bhqk", grad_f, value_f)
    row_dots = jnp.transpose(jnp.sum(grad_f * mixed, -1), (0, 2, 1))[..., None]
    grad_scores = to_low(weights * (grad_weights - row_dots))
    query_grad = (jnp.einsum("bhqk,bkhd->bqhd", grad_scores, key_f) * score_scale).astype(jnp.bfloat16)
    key_grad = jnp.einsum("bhqk,bqhd->bkhd", grad_scores, query_f) * score_scale
    value_grad = jnp.einsum("bhqk,bqhd->bkhd", weights_low, grad_f)
    return mixed.astype(jnp.bfloat16), query_grad, key_grad, value_grad


def reference(queries, key_rows, value_rows, out_grads, neighbours):
    patches = neighbours.shape[0]
    shape_four = (patches, PATCH, HEADS, HEAD_DIM)
    query_four = queries.reshape(shape_four)
    key_four = key_rows.reshape(shape_four)
    value_four = value_rows.reshape(shape_four)
    grad_four = out_grads.reshape(shape_four)
    key_index = jnp.concatenate([jnp.arange(patches, dtype=jnp.int32)[:, None], neighbours.astype(jnp.int32)], 1)
    block = math.gcd(patches, max(1, 512 // PATCH))
    block_count = patches // block
    span = (NBRS + 1) * PATCH

    def one_block(carry, inputs):
        key_acc, value_acc = carry
        query_blk, grad_blk, index_blk = inputs
        flat_index = index_blk.reshape(-1)
        key_blk = jnp.take(key_four, flat_index, axis=0).reshape(block, span, HEADS, HEAD_DIM)
        value_blk = jnp.take(value_four, flat_index, axis=0).reshape(block, span, HEADS, HEAD_DIM)
        mixed, query_grad, key_grad, value_grad = attend_block(query_blk, grad_blk, key_blk, value_blk)
        key_acc = key_acc.at[flat_index].add(key_grad.reshape(block * (NBRS + 1), PATCH, HEADS, HEAD_DIM))
        value_acc = value_acc.at[flat_index].add(value_grad.reshape(block * (NBRS + 1), PATCH, HEADS, HEAD_DIM))
        return (key_acc, value_acc), (mixed, query_grad)

    zeros_acc = jnp.zeros(shape_four, jnp.float32)
    inputs = (query_four.reshape(block_count, block, PATCH, HEADS, HEAD_DIM),
              grad_four.reshape(block_count, block, PATCH, HEADS, HEAD_DIM),
              key_index.reshape(block_count, block, NBRS + 1))
    (key_acc, value_acc), (mixed_all, qgrad_all) = lax.scan(one_block, (zeros_acc, zeros_acc), inputs)
    total = patches * PATCH
    width = HEADS * HEAD_DIM
    return (mixed_all.reshape(total, width), qgrad_all.reshape(total, width),
            key_acc.reshape(total, width).astype(jnp.bfloat16), value_acc.reshape(total, width).astype(jnp.bfloat16))
```

```python
import functools
import math

import jax
import jax.numpy as jnp
from jax import lax
from jax.experimental import pallas as pl
from jax.experimental.pallas import tpu as pltpu
from jax.sharding import PartitionSpec as P

HEAD_DIM = 64
NEVER = -1e30
VMEM = pl.BlockSpec(memory_space=pltpu.VMEM)
SMEM = pl.BlockSpec(memory_space=pltpu.SMEM)
ANY = pl.BlockSpec(memory_space=pl.ANY)
NT = (((1,), (1,)), ((), ()))


def dot(left, right, dims=(((1,), (0,)), ((), ()))):
    return lax.dot_general(left, right, dims, preferred_element_type=jnp.float32)


def partners(node, owners):
    odd = lax.rem(node, 2)
    return node + 1 - 2 * odd, node - 1 + 2 * odd


def pair_routes(owners):
    first = [(i, i ^ 1 if i ^ 1 < owners else i) for i in range(owners)]
    other = [i - 1 + 2 * (i % 2) for i in range(owners)]
    second = [(i, j if 0 <= j < owners else i) for i, j in enumerate(other)]
    return first, second


def wanted(nbr_ref, partner, node, local_count, owners):
    inside = jnp.logical_and(partner >= 0, partner < owners)
    row = jnp.where(inside, partner, 0) * local_count
    found = jnp.int32(0)
    for p in range(local_count):
        for j in range(nbr_ref.shape[1]):
            entry = nbr_ref[row + p, j] - node * local_count
            mine = jnp.logical_and(entry >= 0, entry < local_count)
            found = jnp.where(jnp.logical_and(inside, mine), entry, found)
    return found


def pack_kernel(heads, width, one_ref, two_ref, *refs):
    outs, sem = refs[:heads], refs[heads]
    me = lax.axis_index("head")
    copies = []
    for d in range(heads):
        cols = pl.ds(pl.multiple_of((me ^ d) * width, width), width)
        for a, ref in enumerate((one_ref, two_ref)):
            copies.append(pltpu.make_async_copy(ref.at[:, cols], outs[d].at[a], sem.at[2 * d + a]))
    for copy in copies:
        copy.start()
    for copy in copies:
        copy.wait()


def unpack_kernel(heads, width, *refs):
    blocks, outs, sem = refs[:heads], refs[heads : heads + 2], refs[heads + 2]
    me = lax.axis_index("head")
    copies = []
    for d in range(heads):
        cols = pl.ds(pl.multiple_of((me ^ d) * width, width), width)
        for a, ref in enumerate(outs):
            copies.append(pltpu.make_async_copy(blocks[d].at[a], ref.at[:, cols], sem.at[2 * d + a]))
    for copy in copies:
        copy.start()
    for copy in copies:
        copy.wait()


def pick_kernel(heads, owners, local_count, nbr_ref, *refs):
    blocks, outs = refs[:heads], refs[heads:]
    rows = blocks[0].shape[1]
    per_patch = outs[0].shape[1] // rows
    me, node = lax.axis_index("head"), lax.axis_index("node")
    for out, partner in zip(outs, partners(node, owners)):
        chosen = wanted(nbr_ref, partner, node, local_count, owners)
        for t in range(per_patch):
            slot = me ^ (chosen * per_patch + t)
            value = blocks[0][...]
            for d in range(1, heads):
                value = jnp.where(slot == d, blocks[d][...], value)
            out[:, t * rows : (t + 1) * rows, :] = value


def attend_kernel(heads, owners, local_count, nbr_ref, *refs):
    kv, qg, far = refs[:heads], refs[heads : 2 * heads], refs[2 * heads : 2 * heads + 2]
    outs = refs[2 * heads + 2 :]
    mq_out, near_out, far_out = outs[:heads], outs[heads : 2 * heads], outs[2 * heads : 2 * heads + 2]
    w_all, ds_all = outs[2 * heads + 2 :]
    rows, width = kv[0].shape[1:]
    patch = far[0].shape[1]
    queries = heads * rows
    groups = width // HEAD_DIM
    me, node = lax.axis_index("head"), lax.axis_index("node")
    pair = partners(node, owners)

    own = [[jnp.int32(p == k) for k in range(local_count)] for p in range(local_count)]
    out_of = [[jnp.int32(0), jnp.int32(0)] for _ in range(local_count)]
    for p in range(local_count):
        for j in range(nbr_ref.shape[1]):
            entry = nbr_ref[node * local_count + p, j]
            for k in range(local_count):
                own[p][k] += jnp.where(entry == node * local_count + k, 1, 0)
            for s in range(2):
                start = pair[s] * local_count
                inside = jnp.logical_and(entry >= start, entry < start + local_count)
                out_of[p][s] += jnp.where(inside, 1, 0)

    def choose(index, values):
        value = values[0]
        for i in range(1, len(values)):
            value = jnp.where(index == i, values[i], value)
        return value

    patch_of = [((me ^ d) * rows) // patch for d in range(heads)]
    lane_block = lax.broadcasted_iota(jnp.int32, (1, queries), 1) // rows
    key_counts = []
    for d in range(heads):
        key_counts.append(
            [choose(patch_of[e], [choose(patch_of[d], own[p]) for p in range(local_count)]) for e in range(heads)]
        )
    for s in range(2):
        key_counts.append([choose(patch_of[e], [out_of[p][s] for p in range(local_count)]) for e in range(heads)])
    biases = []
    for counts in key_counts:
        row = jnp.zeros((1, queries), jnp.float32)
        for e in range(heads):
            row = jnp.where(lane_block == e, counts[e].astype(jnp.float32), row)
        biases.append(jnp.where(row > 0.5, jnp.log(jnp.maximum(row, 1.0)) * (1 / math.log(2)), NEVER))
    sizes = [rows] * heads + [patch, patch]
    bias = jnp.concatenate([jnp.broadcast_to(b, (n, queries)) for b, n in zip(biases, sizes)], 0)

    keys = jnp.concatenate([r[0] for r in kv] + [r[0] for r in far], 0)
    values = jnp.concatenate([r[1] for r in kv] + [r[1] for r in far], 0)
    query = jnp.concatenate([r[0] for r in qg], 0)
    grad = jnp.concatenate([r[1] for r in qg], 0)
    keys_t, values_t = keys.T, values.T
    lane_head = lax.broadcasted_iota(jnp.int32, (1, width), 1) // HEAD_DIM
    scale = HEAD_DIM**-0.5
    mixed_t, qgrad_t, query_h, grad_h = [], [], [], []
    for head in range(groups):
        feats = slice(head * HEAD_DIM, (head + 1) * HEAD_DIM)
        lanes = slice(head * queries, (head + 1) * queries)
        query_h.append(jnp.where(lane_head == head, query, jnp.zeros_like(query)))
        grad_h.append(jnp.where(lane_head == head, grad, jnp.zeros_like(grad)))
        scores = dot(keys, query_h[head], NT) * (scale / math.log(2)) + bias
        weights = jnp.exp2(scores - jnp.max(scores, 0, keepdims=True))
        weights = weights * (1.0 / jnp.sum(weights, 0, keepdims=True))
        weights_low = weights.astype(jnp.bfloat16)
        grad_weights = dot(values, grad_h[head], NT)
        row_dots = jnp.sum(weights * grad_weights, 0, keepdims=True)
        grad_scores = (weights * (grad_weights - row_dots)).astype(jnp.bfloat16)
        w_all[:, lanes] = weights_low
        ds_all[:, lanes] = grad_scores
        mixed_t.append(dot(values_t[feats], weights_low))
        qgrad_t.append(dot(keys_t[feats], grad_scores) * scale)
    mixed = jnp.concatenate(mixed_t, 0).T.astype(jnp.bfloat16)
    qgrad = jnp.concatenate(qgrad_t, 0).T.astype(jnp.bfloat16)
    key_grad = dot(ds_all[...], jnp.concatenate(query_h, 0)) * scale
    value_grad = dot(w_all[...], jnp.concatenate(grad_h, 0))
    for d in range(heads):
        span = slice(d * rows, (d + 1) * rows)
        mq_out[d][0], mq_out[d][1] = mixed[span], qgrad[span]
        near_out[d][0], near_out[d][1] = key_grad[span], value_grad[span]
    for s in range(2):
        span = slice(queries + s * patch, queries + (s + 1) * patch)
        far_out[s][0], far_out[s][1] = key_grad[span].astype(jnp.bfloat16), value_grad[span].astype(jnp.bfloat16)


def merge_kernel(heads, owners, local_count, nbr_ref, *refs):
    near, back, outs = refs[:heads], refs[heads : heads + 2], refs[heads + 2 :]
    rows = near[0].shape[1]
    per_patch = back[0].shape[1] // rows
    me, node = lax.axis_index("head"), lax.axis_index("node")
    chosen = [wanted(nbr_ref, partner, node, local_count, owners) for partner in partners(node, owners)]
    for d in range(heads):
        total = near[d][...]
        for s in range(2):
            slot = me ^ d
            for t in range(per_patch):
                hit = slot == chosen[s] * per_patch + t
                term = back[s][:, t * rows : (t + 1) * rows, :].astype(jnp.float32)
                total = total + jnp.where(hit, term, 0.0)
        outs[d][...] = total.astype(jnp.bfloat16)


def exchange(blocks):
    heads = len(blocks)
    return [blocks[0]] + [
        lax.ppermute(blocks[d], "head", [(i, i ^ d) for i in range(heads)]) for d in range(1, heads)
    ]


def shards(queries, key_rows, value_rows, out_grads, neighbours):
    rows, features = queries.shape
    heads, owners = lax.axis_size("head"), lax.axis_size("node")
    width = features // heads
    local_count = neighbours.shape[0] // owners
    patch = rows * heads // local_count
    low = jnp.bfloat16
    block = jax.ShapeDtypeStruct((2, rows, width), low)
    wide = jax.ShapeDtypeStruct((2, rows, width), jnp.float32)
    slab = jax.ShapeDtypeStruct((2, patch, width), low)
    sems = [pltpu.SemaphoreType.DMA((2 * heads,))]
    routes = pair_routes(owners)

    def pack(one, two):
        return pl.pallas_call(
            functools.partial(pack_kernel, heads, width),
            out_shape=[block] * heads,
            in_specs=[ANY] * 2,
            out_specs=[ANY] * heads,
            scratch_shapes=sems,
            name="pack",
        )(one, two)

    def unpack(blocks):
        return pl.pallas_call(
            functools.partial(unpack_kernel, heads, width),
            out_shape=[jax.ShapeDtypeStruct((rows, features), low)] * 2,
            in_specs=[ANY] * heads,
            out_specs=[ANY] * 2,
            scratch_shapes=sems,
            name="unpack",
        )(*blocks)

    kv = exchange(pack(key_rows, value_rows))
    qg = exchange(pack(queries, out_grads))
    picked = pl.pallas_call(
        functools.partial(pick_kernel, heads, owners, local_count),
        out_shape=[slab] * 2,
        in_specs=[SMEM] + [VMEM] * heads,
        out_specs=[VMEM] * 2,
        name="pick",
    )(neighbours, *kv)
    far = [lax.ppermute(p, "node", r) for p, r in zip(picked, routes)]
    results = pl.pallas_call(
        functools.partial(attend_kernel, heads, owners, local_count),
        out_shape=[block] * heads + [wide] * heads + [slab] * 2,
        in_specs=[SMEM] + [VMEM] * (2 * heads + 2),
        out_specs=[VMEM] * (2 * heads + 2),
        scratch_shapes=[
            pltpu.VMEM((heads * rows + 2 * patch, width // HEAD_DIM * heads * rows), low),
            pltpu.VMEM((heads * rows + 2 * patch, width // HEAD_DIM * heads * rows), low),
        ],
        name="attend",
        compiler_params=pltpu.CompilerParams(vmem_limit_bytes=32 * 1024 * 1024),
    )(neighbours, *kv, *qg, *far)
    mq, near, far_grads = results[:heads], results[heads : 2 * heads], results[2 * heads :]
    back = [lax.ppermute(p, "node", r) for p, r in zip(far_grads, routes)]
    merged = pl.pallas_call(
        functools.partial(merge_kernel, heads, owners, local_count),
        out_shape=[block] * heads,
        in_specs=[SMEM] + [VMEM] * (heads + 2),
        out_specs=[VMEM] * heads,
        name="merge",
    )(neighbours, *near, *back)
    mixed, query_grad = unpack(exchange(mq))
    key_grad, value_grad = unpack(exchange(merged))
    return mixed, query_grad, key_grad, value_grad


def solution(mesh):
    rows = P(("grp", "node", "head"), None)
    return jax.shard_map(
        shards,
        mesh=mesh,
        in_specs=(rows, rows, rows, rows, P("grp", None)),
        out_specs=(rows, rows, rows, rows),
        check_vma=False,
    )
```

```python
import functools
import math

import jax
import jax.numpy as jnp
from jax import lax
from jax.experimental import pallas as pl
from jax.experimental.pallas import tpu as pltpu
from jax.sharding import PartitionSpec as P

HEAD_DIM = 64
NEVER = -1e30
VMEM = pl.BlockSpec(memory_space=pltpu.VMEM)
SMEM = pl.BlockSpec(memory_space=pltpu.SMEM)
SMALL = pltpu.CompilerParams(vmem_limit_bytes=8 * 1024 * 1024)
NT = (((1,), (1,)), ((), ()))


def dot(left, right, dims=(((1,), (0,)), ((), ()))):
    return lax.dot_general(left, right, dims, preferred_element_type=jnp.float32)


def partners(node, owners):
    odd = lax.rem(node, 2)
    return node + 1 - 2 * odd, node - 1 + 2 * odd


def pair_routes(owners):
    first = [(i, i ^ 1 if i ^ 1 < owners else i) for i in range(owners)]
    other = [i - 1 + 2 * (i % 2) for i in range(owners)]
    second = [(i, j if 0 <= j < owners else i) for i, j in enumerate(other)]
    return first, second


def wanted(nbr_ref, partner, node, local_count, owners):
    inside = jnp.logical_and(partner >= 0, partner < owners)
    row = jnp.where(inside, partner, 0) * local_count
    found = jnp.int32(0)
    for p in range(local_count):
        for j in range(nbr_ref.shape[1]):
            entry = nbr_ref[row + p, j] - node * local_count
            mine = jnp.logical_and(entry >= 0, entry < local_count)
            found = jnp.where(jnp.logical_and(inside, mine), entry, found)
    return found


def pack_kernel(heads, width, one_ref, two_ref, *outs):
    me = lax.axis_index("head")
    for d, out in enumerate(outs):
        cols = pl.ds(pl.multiple_of((me ^ d) * width, width), width)
        out[0], out[1] = one_ref[:, cols], two_ref[:, cols]


def unpack_kernel(heads, width, *refs):
    blocks, outs = refs[:heads], refs[heads:]
    me = lax.axis_index("head")
    for d, block in enumerate(blocks):
        cols = pl.ds(pl.multiple_of((me ^ d) * width, width), width)
        for a, out in enumerate(outs):
            out[:, cols] = block[a]


def pick_kernel(heads, owners, local_count, nbr_ref, *refs):
    blocks, outs = refs[:heads], refs[heads:]
    rows = blocks[0].shape[1]
    per_patch = outs[0].shape[1] // rows
    me, node = lax.axis_index("head"), lax.axis_index("node")
    for out, partner in zip(outs, partners(node, owners)):
        chosen = wanted(nbr_ref, partner, node, local_count, owners)
        for t in range(per_patch):
            slot = me ^ (chosen * per_patch + t)
            value = blocks[0][...]
            for d in range(1, heads):
                value = jnp.where(slot == d, blocks[d][...], value)
            out[:, t * rows : (t + 1) * rows, :] = value


def attend_kernel(heads, owners, local_count, nbr_ref, *refs):
    kv, qg, far = refs[:heads], refs[heads : 2 * heads], refs[2 * heads : 2 * heads + 2]
    outs = refs[2 * heads + 2 :]
    mq_out, near_out, far_out = outs[:heads], outs[heads : 2 * heads], outs[2 * heads : 2 * heads + 2]
    w_all, ds_all = outs[2 * heads + 2 :]
    rows, width = kv[0].shape[1:]
    patch = far[0].shape[1]
    queries = heads * rows
    groups = width // HEAD_DIM
    me, node = lax.axis_index("head"), lax.axis_index("node")
    pair = partners(node, owners)

    own = [[jnp.int32(p == k) for k in range(local_count)] for p in range(local_count)]
    out_of = [[jnp.int32(0), jnp.int32(0)] for _ in range(local_count)]
    for p in range(local_count):
        for j in range(nbr_ref.shape[1]):
            entry = nbr_ref[node * local_count + p, j]
            for k in range(local_count):
                own[p][k] += jnp.where(entry == node * local_count + k, 1, 0)
            for s in range(2):
                start = pair[s] * local_count
                inside = jnp.logical_and(entry >= start, entry < start + local_count)
                out_of[p][s] += jnp.where(inside, 1, 0)

    def choose(index, values):
        value = values[0]
        for i in range(1, len(values)):
            value = jnp.where(index == i, values[i], value)
        return value

    patch_of = [((me ^ d) * rows) // patch for d in range(heads)]
    lane_block = lax.broadcasted_iota(jnp.int32, (1, queries), 1) // rows
    key_counts = []
    for d in range(heads):
        key_counts.append(
            [choose(patch_of[e], [choose(patch_of[d], own[p]) for p in range(local_count)]) for e in range(heads)]
        )
    for s in range(2):
        key_counts.append([choose(patch_of[e], [out_of[p][s] for p in range(local_count)]) for e in range(heads)])
    biases = []
    for counts in key_counts:
        row = jnp.zeros((1, queries), jnp.float32)
        for e in range(heads):
            row = jnp.where(lane_block == e, counts[e].astype(jnp.float32), row)
        biases.append(jnp.where(row > 0.5, jnp.log(jnp.maximum(row, 1.0)) * (1 / math.log(2)), NEVER))
    sizes = [rows] * heads + [patch, patch]
    bias = jnp.concatenate([jnp.broadcast_to(b, (n, queries)) for b, n in zip(biases, sizes)], 0)

    keys = jnp.concatenate([r[0] for r in kv] + [r[0] for r in far], 0)
    values = jnp.concatenate([r[1] for r in kv] + [r[1] for r in far], 0)
    query = jnp.concatenate([r[0] for r in qg], 0)
    grad = jnp.concatenate([r[1] for r in qg], 0)
    keys_t, values_t = keys.T, values.T
    lane_head = lax.broadcasted_iota(jnp.int32, (1, width), 1) // HEAD_DIM
    scale = HEAD_DIM**-0.5
    mixed_t, qgrad_t, query_h, grad_h = [], [], [], []
    for head in range(groups):
        feats = slice(head * HEAD_DIM, (head + 1) * HEAD_DIM)
        lanes = slice(head * queries, (head + 1) * queries)
        query_h.append(jnp.where(lane_head == head, query, jnp.zeros_like(query)))
        grad_h.append(jnp.where(lane_head == head, grad, jnp.zeros_like(grad)))
        scores = dot(keys, query_h[head], NT) * (scale / math.log(2)) + bias
        weights = jnp.exp2(scores - jnp.max(scores, 0, keepdims=True))
        weights = weights * (1.0 / jnp.sum(weights, 0, keepdims=True))
        weights_low = weights.astype(jnp.bfloat16)
        grad_weights = dot(values, grad_h[head], NT)
        row_dots = jnp.sum(weights * grad_weights, 0, keepdims=True)
        grad_scores = (weights * (grad_weights - row_dots)).astype(jnp.bfloat16)
        w_all[:, lanes] = weights_low
        ds_all[:, lanes] = grad_scores
        mixed_t.append(dot(values_t[feats], weights_low))
        qgrad_t.append(dot(keys_t[feats], grad_scores) * scale)
    mixed = jnp.concatenate(mixed_t, 0).T.astype(jnp.bfloat16)
    qgrad = jnp.concatenate(qgrad_t, 0).T.astype(jnp.bfloat16)
    key_grad = dot(ds_all[...], jnp.concatenate(query_h, 0)) * scale
    value_grad = dot(w_all[...], jnp.concatenate(grad_h, 0))
    for d in range(heads):
        span = slice(d * rows, (d + 1) * rows)
        mq_out[d][0], mq_out[d][1] = mixed[span], qgrad[span]
        near_out[d][0], near_out[d][1] = key_grad[span], value_grad[span]
    for s in range(2):
        span = slice(queries + s * patch, queries + (s + 1) * patch)
        far_out[s][0], far_out[s][1] = key_grad[span].astype(jnp.bfloat16), value_grad[span].astype(jnp.bfloat16)


def merge_kernel(heads, owners, local_count, nbr_ref, *refs):
    near, back, outs = refs[:heads], refs[heads : heads + 2], refs[heads + 2 :]
    rows = near[0].shape[1]
    per_patch = back[0].shape[1] // rows
    me, node = lax.axis_index("head"), lax.axis_index("node")
    chosen = [wanted(nbr_ref, partner, node, local_count, owners) for partner in partners(node, owners)]
    for d in range(heads):
        total = near[d][...]
        for s in range(2):
            slot = me ^ d
            for t in range(per_patch):
                hit = slot == chosen[s] * per_patch + t
                term = back[s][:, t * rows : (t + 1) * rows, :].astype(jnp.float32)
                total = total + jnp.where(hit, term, 0.0)
        outs[d][...] = total.astype(jnp.bfloat16)


def exchange(blocks):
    heads = len(blocks)
    return [blocks[0]] + [
        lax.ppermute(blocks[d], "head", [(i, i ^ d) for i in range(heads)]) for d in range(1, heads)
    ]


def shards(queries, key_rows, value_rows, out_grads, neighbours):
    rows, features = queries.shape
    heads, owners = lax.axis_size("head"), lax.axis_size("node")
    width = features // heads
    local_count = neighbours.shape[0] // owners
    patch = rows * heads // local_count
    low = jnp.bfloat16
    block = jax.ShapeDtypeStruct((2, rows, width), low)
    wide = jax.ShapeDtypeStruct((2, rows, width), jnp.float32)
    slab = jax.ShapeDtypeStruct((2, patch, width), low)
    routes = pair_routes(owners)

    def pack(one, two):
        return pl.pallas_call(
            functools.partial(pack_kernel, heads, width),
            out_shape=[block] * heads,
            in_specs=[VMEM] * 2,
            out_specs=[VMEM] * heads,
            name="pack",
            compiler_params=SMALL,
        )(one, two)

    def unpack(blocks):
        return pl.pallas_call(
            functools.partial(unpack_kernel, heads, width),
            out_shape=[jax.ShapeDtypeStruct((rows, features), low)] * 2,
            in_specs=[VMEM] * heads,
            out_specs=[VMEM] * 2,
            name="unpack",
            compiler_params=SMALL,
        )(*blocks)

    kv = exchange(pack(key_rows, value_rows))
    qg = exchange(pack(queries, out_grads))
    picked = pl.pallas_call(
        functools.partial(pick_kernel, heads, owners, local_count),
        out_shape=[slab] * 2,
        in_specs=[SMEM] + [VMEM] * heads,
        out_specs=[VMEM] * 2,
        name="pick",
        compiler_params=SMALL,
    )(neighbours, *kv)
    far = [lax.ppermute(p, "node", r) for p, r in zip(picked, routes)]
    results = pl.pallas_call(
        functools.partial(attend_kernel, heads, owners, local_count),
        out_shape=[block] * heads + [wide] * heads + [slab] * 2,
        in_specs=[SMEM] + [VMEM] * (2 * heads + 2),
        out_specs=[VMEM] * (2 * heads + 2),
        scratch_shapes=[
            pltpu.VMEM((heads * rows + 2 * patch, width // HEAD_DIM * heads * rows), low),
            pltpu.VMEM((heads * rows + 2 * patch, width // HEAD_DIM * heads * rows), low),
        ],
        name="attend",
        compiler_params=pltpu.CompilerParams(vmem_limit_bytes=24 * 1024 * 1024),
    )(neighbours, *kv, *qg, *far)
    mq, near, far_grads = results[:heads], results[heads : 2 * heads], results[2 * heads :]
    back = [lax.ppermute(p, "node", r) for p, r in zip(far_grads, routes)]
    merged = pl.pallas_call(
        functools.partial(merge_kernel, heads, owners, local_count),
        out_shape=[block] * heads,
        in_specs=[SMEM] + [VMEM] * (heads + 2),
        out_specs=[VMEM] * heads,
        name="merge",
        compiler_params=SMALL,
    )(neighbours, *near, *back)
    mixed, query_grad = unpack(exchange(mq))
    key_grad, value_grad = unpack(exchange(merged))
    return mixed, query_grad, key_grad, value_grad


def solution(mesh):
    rows = P(("grp", "node", "head"), None)
    return jax.shard_map(
        shards,
        mesh=mesh,
        in_specs=(rows, rows, rows, rows, P("grp", None)),
        out_specs=(rows, rows, rows, rows),
        check_vma=False,
    )
```

```python
import functools
import math

import jax
import jax.numpy as jnp
from jax import lax
from jax.experimental import pallas as pl
from jax.experimental.pallas import tpu as pltpu
from jax.sharding import PartitionSpec as P

HEAD_DIM = 64
NEVER = -1e30
LOW = jnp.bfloat16
VMEM = pl.BlockSpec(memory_space=pltpu.VMEM)
SMEM = pl.BlockSpec(memory_space=pltpu.SMEM)
NT = (((1,), (1,)), ((), ()))


def dot(left, right, dims=(((1,), (0,)), ((), ()))):
    return lax.dot_general(left, right, dims, preferred_element_type=jnp.float32)


def call(kernel, name, outs, *args, limit=8, scratch=(), cost=None, specs=None):
    return pl.pallas_call(
        kernel,
        out_shape=outs,
        in_specs=specs or [VMEM] * len(args),
        out_specs=[VMEM] * len(outs),
        scratch_shapes=scratch,
        name=name,
        cost_estimate=cost,
        compiler_params=pltpu.CompilerParams(vmem_limit_bytes=limit * 1024 * 1024),
    )(*args)


def pair_routes(owners, heads):
    routes = []
    for step in (1, -1):
        route = []
        for n in range(owners):
            other = n + step * (1 - 2 * (n % 2))
            for h in range(heads):
                target = other * heads + h if 0 <= other < owners else n * heads + (h ^ 1)
                route.append((n * heads + h, target))
        routes.append(route)
    return routes


def prep_kernel(heads, owners, local_count, per_patch, rows, nbr_ref, after_ref, bias_ref, slot_ref):
    me, node = lax.axis_index("head"), lax.axis_index("node")
    odd = lax.rem(node, 2)
    pair = (node + 1 - 2 * odd, node - 1 + 2 * odd)
    queries = heads * rows
    own = [[jnp.int32(p == k) for k in range(local_count)] for p in range(local_count)]
    out_of = [[jnp.int32(0), jnp.int32(0)] for _ in range(local_count)]
    for p in range(local_count):
        for j in range(nbr_ref.shape[1]):
            entry = nbr_ref[node * local_count + p, j]
            for k in range(local_count):
                own[p][k] += jnp.where(entry == node * local_count + k, 1, 0)
            for s in range(2):
                start = pair[s] * local_count
                inside = jnp.logical_and(entry >= start, entry < start + local_count)
                out_of[p][s] += jnp.where(inside, 1, 0)

    def choose(index, values):
        value = values[0]
        for i in range(1, len(values)):
            value = jnp.where(index == i, values[i], value)
        return value

    patch_of = [(me ^ d) // per_patch for d in range(heads)]
    counts = [
        [choose(patch_of[e], [choose(patch_of[d], own[p]) for p in range(local_count)]) for e in range(heads)]
        for d in range(heads)
    ]
    for s in range(2):
        counts.append([choose(patch_of[e], [out_of[p][s] for p in range(local_count)]) for e in range(heads)])
    lane_block = lax.broadcasted_iota(jnp.int32, (1, queries), 1) // rows
    for b, row_counts in enumerate(counts):
        row = jnp.zeros((1, queries), jnp.float32)
        for e in range(heads):
            row = jnp.where(lane_block == e, row_counts[e].astype(jnp.float32), row)
        row = jnp.where(row > 0.5, jnp.log(jnp.maximum(row, 1.0)) * (1 / math.log(2)), NEVER)
        bias_ref[b : b + 1, :] = row
    for s in range(2):
        inside = jnp.logical_and(pair[s] >= 0, pair[s] < owners)
        first = jnp.where(inside, pair[s], 0) * local_count
        chosen = jnp.int32(0)
        for p in range(local_count):
            for j in range(nbr_ref.shape[1]):
                entry = nbr_ref[first + p, j] - node * local_count
                mine = jnp.logical_and(entry >= 0, entry < local_count)
                chosen = jnp.where(jnp.logical_and(inside, mine), entry, chosen)
        for t in range(per_patch):
            slot = me ^ (chosen * per_patch + t)
            slot_ref[s * per_patch + t : s * per_patch + t + 1, :] = jnp.full((1, slot_ref.shape[1]), slot)


def pack_kernel(heads, keys, both_ref, one_peer, two_peer, *refs):
    me = lax.axis_index("head")
    outs = refs[-len(keys) :]
    width = outs[0].shape[-1]
    for out, pairs in zip(outs, keys):
        for i, (u, w) in enumerate(pairs):
            one, two = (one_peer, two_peer) if u else (both_ref.at[0], both_ref.at[1])
            cols = pl.ds(pl.multiple_of((me ^ w) * width, width), width)
            out[i, 0], out[i, 1] = one[:, cols], two[:, cols]


def gather_kernel(places, *refs):
    for i, (a, j) in enumerate(places):
        refs[-1][i] = refs[a][j]


def pick_kernel(heads, places, slot_ref, *refs):
    arrays, outs = refs[:-2], refs[-2:]
    rows = arrays[0].shape[2]
    per_patch = outs[0].shape[1] // rows
    blocks = [arrays[a][j].astype(jnp.float32) for a, j in places]
    for s, out in enumerate(outs):
        for t in range(per_patch):
            slot = slot_ref[s * per_patch + t : s * per_patch + t + 1, :]
            value = blocks[0]
            for d in range(1, heads):
                value = jnp.where((slot == d)[None], blocks[d], value)
            out[:, t * rows : (t + 1) * rows, :] = value.astype(LOW)


def attend_kernel(heads, places, count, bias_ref, *refs):
    kv_arrays, qg_arrays, far, outs = refs[:count], refs[count : 2 * count], refs[2 * count : 2 * count + 2], refs[2 * count + 2 :]
    mq_kept, mq_sent, near_out, far_a, far_b, w_all, ds_all = outs
    kv = [kv_arrays[a].at[j] for a, j in places]
    qg = [qg_arrays[a].at[j] for a, j in places]
    rows, width = kv[0].shape[1:]
    patch = far[0].shape[1]
    queries = heads * rows
    groups = width // HEAD_DIM
    sizes = [rows] * heads + [patch, patch]
    bias = jnp.concatenate(
        [jnp.broadcast_to(bias_ref[b : b + 1, :], (n, queries)) for b, n in enumerate(sizes)], 0
    )
    keys = jnp.concatenate([r[0] for r in kv] + [r[0] for r in far], 0)
    values = jnp.concatenate([r[1] for r in kv] + [r[1] for r in far], 0)
    query = jnp.concatenate([r[0] for r in qg], 0)
    grad = jnp.concatenate([r[1] for r in qg], 0)
    keys_t, values_t = keys.T, values.T
    lane_head = lax.broadcasted_iota(jnp.int32, (1, width), 1) // HEAD_DIM
    scale = HEAD_DIM**-0.5
    mixed_t, qgrad_t, query_h, grad_h = [], [], [], []
    for head in range(groups):
        feats = slice(head * HEAD_DIM, (head + 1) * HEAD_DIM)
        lanes = slice(head * queries, (head + 1) * queries)
        query_h.append(jnp.where(lane_head == head, query, jnp.zeros_like(query)))
        grad_h.append(jnp.where(lane_head == head, grad, jnp.zeros_like(grad)))
        scores = dot(keys, query_h[head], NT) * (scale / math.log(2)) + bias
        weights = jnp.exp2(scores - jnp.max(scores, 0, keepdims=True))
        weights = weights * (1.0 / jnp.sum(weights, 0, keepdims=True))
        weights_low = weights.astype(LOW)
        grad_weights = dot(values, grad_h[head], NT)
        row_dots = jnp.sum(weights * grad_weights, 0, keepdims=True)
        grad_scores = (weights * (grad_weights - row_dots)).astype(LOW)
        w_all[:, lanes] = weights_low
        ds_all[:, lanes] = grad_scores
        mixed_t.append(dot(values_t[feats], weights_low))
        qgrad_t.append(dot(keys_t[feats], grad_scores) * scale)
    mixed = jnp.concatenate(mixed_t, 0).T.astype(LOW)
    qgrad = jnp.concatenate(qgrad_t, 0).T.astype(LOW)
    key_grad = dot(ds_all[...], jnp.concatenate(query_h, 0)) * scale
    value_grad = dot(w_all[...], jnp.concatenate(grad_h, 0))
    for d in range(heads):
        span = slice(d * rows, (d + 1) * rows)
        out = (mq_sent if d % 2 else mq_kept).at[d // 2]
        out[0], out[1] = mixed[span], qgrad[span]
        near_out[d, 0], near_out[d, 1] = key_grad[span], value_grad[span]
    for s, out in enumerate((far_a, far_b)):
        span = slice(queries + s * patch, queries + (s + 1) * patch)
        out[0], out[1] = key_grad[span].astype(LOW), value_grad[span].astype(LOW)


def merge_kernel(heads, slot_ref, near, back_a, back_b, kept, sent):
    rows = near.shape[2]
    per_patch = back_a.shape[1] // rows
    for d in range(heads):
        total = near[d]
        for s, back in enumerate((back_a, back_b)):
            for t in range(per_patch):
                slot = slot_ref[s * per_patch + t : s * per_patch + t + 1, :]
                term = back[:, t * rows : (t + 1) * rows, :].astype(jnp.float32)
                total = total + jnp.where((slot == d)[None], term, 0.0)
        (sent if d % 2 else kept)[d // 2] = total.astype(LOW)


def unpack_kernel(heads, places, *refs):
    arrays, outs = refs[:-2], refs[-2:]
    width = arrays[0].shape[-1]
    me = lax.axis_index("head")
    for d, (a, j) in enumerate(places):
        cols = pl.ds(pl.multiple_of((me ^ d) * width, width), width)
        outs[0][:, cols], outs[1][:, cols] = arrays[a][j, 0], arrays[a][j, 1]


def swap(array, bit):
    heads = lax.axis_size("head")
    return lax.ppermute(array, "head", [(i, i ^ bit) for i in range(heads)])


def regroup(arrays, places):
    shape = jax.ShapeDtypeStruct((len(places),) + arrays[0].shape[1:], LOW)
    return call(functools.partial(gather_kernel, places), "regroup", [shape], *arrays)[0]


def exchange(heads, bit, arrays, held, outgoing, going):
    while True:
        arrays.append(swap(outgoing, bit))
        for i, (u, w) in enumerate(going):
            held[(u + bit, w - bit)] = (len(arrays) - 1, i)
        bit *= 2
        if bit >= heads:
            return arrays, [held[(d, 0)] for d in range(heads)]
        going = sorted(k for k in held if k[1] & bit)
        outgoing = regroup(arrays, [held.pop(k) for k in going])


def gather_in(heads, one, two, block, *after):
    one_peer, two_peer = swap(one, 1), swap(two, 1)
    both = lax.optimization_barrier(jnp.concatenate([one, two], 0)).reshape((2,) + one.shape)
    keys = [[(u, w) for u in range(2) for w in range(0, heads, 2) if bool(w & 2) == b] for b in (False, True)]
    shapes = [jax.ShapeDtypeStruct((len(k),) + block, LOW) for k in keys]
    kept, sent = call(functools.partial(pack_kernel, heads, keys), "pack", shapes, both, one_peer, two_peer, *after)
    held = {k: (0, i) for i, k in enumerate(keys[0])}
    return exchange(heads, 2, [kept], held, sent, keys[1])


def scatter_out(heads, kept, sent):
    held = {(0, w): (0, w // 2) for w in range(0, heads, 2)}
    return exchange(heads, 1, [kept], held, sent, [(0, w) for w in range(1, heads, 2)])


def shards(queries, key_rows, value_rows, out_grads, neighbours):
    rows, features = queries.shape
    heads, owners = lax.axis_size("head"), lax.axis_size("node")
    width = features // heads
    local_count = neighbours.shape[0] // owners
    per_patch = heads // local_count
    patch = rows * per_patch
    half = jax.ShapeDtypeStruct((heads // 2, 2, rows, width), LOW)
    near_shape = jax.ShapeDtypeStruct((heads, 2, rows, width), jnp.float32)
    slab = jax.ShapeDtypeStruct((2, patch, width), LOW)
    whole = jax.ShapeDtypeStruct((rows, features), LOW)
    routes = pair_routes(owners, heads)
    span = heads * rows + 2 * patch
    lanes = width // HEAD_DIM * heads * rows

    kv, places = gather_in(heads, key_rows, value_rows, (2, rows, width))
    bias, slots = call(
        functools.partial(prep_kernel, heads, owners, local_count, per_patch, rows),
        "prep",
        [
            jax.ShapeDtypeStruct((heads + 2, heads * rows), jnp.float32),
            jax.ShapeDtypeStruct((2 * per_patch, width), jnp.int32),
        ],
        neighbours,
        kv[0],
        specs=[SMEM, VMEM],
    )
    qg, _ = gather_in(heads, queries, out_grads, (2, rows, width), slots)
    picked = call(functools.partial(pick_kernel, heads, places), "pick", [slab] * 2, slots, *kv)
    far = [lax.ppermute(p, ("node", "head"), r) for p, r in zip(picked, routes)]
    mq_kept, mq_sent, near, *far_grads = call(
        functools.partial(attend_kernel, heads, places, len(kv)),
        "attend",
        [half, half, near_shape, slab, slab],
        bias,
        *kv,
        *qg,
        *far,
        limit=24,
        scratch=[pltpu.VMEM((span, lanes), LOW)] * 2,
    )
    back = [lax.ppermute(p, ("node", "head"), r) for p, r in zip(far_grads, routes)]
    mq, _ = scatter_out(heads, mq_kept, mq_sent)
    merged = call(functools.partial(merge_kernel, heads), "merge", [half] * 2, slots, near, *back)
    kv_grads, out_places = scatter_out(heads, *merged)
    unpack = functools.partial(unpack_kernel, heads, out_places)
    mixed, query_grad = call(unpack, "unpack", [whole] * 2, *mq)
    key_grad, value_grad = call(unpack, "unpack", [whole] * 2, *kv_grads)
    return mixed, query_grad, key_grad, value_grad


def solution(mesh):
    rows = P(("grp", "node", "head"), None)
    return jax.shard_map(
        shards,
        mesh=mesh,
        in_specs=(rows, rows, rows, rows, P("grp", None)),
        out_specs=(rows, rows, rows, rows),
        check_vma=False,
    )
```

```python
import functools
import math

import jax
import jax.numpy as jnp
from jax import lax
from jax.experimental import pallas as pl
from jax.experimental.pallas import tpu as pltpu
from jax.sharding import PartitionSpec as P

HEAD_DIM = 64
NEVER = -1e30
LOW = jnp.bfloat16
VMEM = pl.BlockSpec(memory_space=pltpu.VMEM)
SMEM = pl.BlockSpec(memory_space=pltpu.SMEM)
NT = (((1,), (1,)), ((), ()))


def dot(left, right, dims=(((1,), (0,)), ((), ()))):
    return lax.dot_general(left, right, dims, preferred_element_type=jnp.float32)


def call(kernel, name, outs, *args, limit=8, scratch=(), cost=None, specs=None):
    return pl.pallas_call(
        kernel,
        out_shape=outs,
        in_specs=specs or [VMEM] * len(args),
        out_specs=[VMEM] * len(outs),
        scratch_shapes=scratch,
        name=name,
        cost_estimate=cost,
        compiler_params=pltpu.CompilerParams(vmem_limit_bytes=limit * 1024 * 1024),
    )(*args)


def all_bits(heads):
    return [1 << i for i in range(heads.bit_length() - 1)]


def split_at(heads, bit):
    return [w for w in range(heads) if not w & bit], [w for w in range(heads) if w & bit]


def pair_routes(owners, heads):
    routes = []
    for step in (1, -1):
        route = []
        for n in range(owners):
            other = n + step * (1 - 2 * (n % 2))
            for h in range(heads):
                target = other * heads + h if 0 <= other < owners else n * heads + (h ^ 1)
                route.append((n * heads + h, target))
        routes.append(route)
    return routes


def prep_kernel(heads, owners, local_count, per_patch, rows, nbr_ref, after_ref, bias_ref, slot_ref):
    me, node = lax.axis_index("head"), lax.axis_index("node")
    odd = lax.rem(node, 2)
    pair = (node + 1 - 2 * odd, node - 1 + 2 * odd)
    queries = heads * rows
    own = [[jnp.int32(p == k) for k in range(local_count)] for p in range(local_count)]
    out_of = [[jnp.int32(0), jnp.int32(0)] for _ in range(local_count)]
    for p in range(local_count):
        for j in range(nbr_ref.shape[1]):
            entry = nbr_ref[node * local_count + p, j]
            for k in range(local_count):
                own[p][k] += jnp.where(entry == node * local_count + k, 1, 0)
            for s in range(2):
                start = pair[s] * local_count
                inside = jnp.logical_and(entry >= start, entry < start + local_count)
                out_of[p][s] += jnp.where(inside, 1, 0)

    def choose(index, values):
        value = values[0]
        for i in range(1, len(values)):
            value = jnp.where(index == i, values[i], value)
        return value

    patch_of = [(me ^ d) // per_patch for d in range(heads)]
    counts = [
        [choose(patch_of[e], [choose(patch_of[d], own[p]) for p in range(local_count)]) for e in range(heads)]
        for d in range(heads)
    ]
    for s in range(2):
        counts.append([choose(patch_of[e], [out_of[p][s] for p in range(local_count)]) for e in range(heads)])
    lane_block = lax.broadcasted_iota(jnp.int32, (1, queries), 1) // rows
    for b, row_counts in enumerate(counts):
        row = jnp.zeros((1, queries), jnp.float32)
        for e in range(heads):
            row = jnp.where(lane_block == e, row_counts[e].astype(jnp.float32), row)
        row = jnp.where(row > 0.5, jnp.log(jnp.maximum(row, 1.0)) * (1 / math.log(2)), NEVER)
        bias_ref[b : b + 1, :] = row
    for s in range(2):
        inside = jnp.logical_and(pair[s] >= 0, pair[s] < owners)
        first = jnp.where(inside, pair[s], 0) * local_count
        chosen = jnp.int32(0)
        for p in range(local_count):
            for j in range(nbr_ref.shape[1]):
                entry = nbr_ref[first + p, j] - node * local_count
                mine = jnp.logical_and(entry >= 0, entry < local_count)
                chosen = jnp.where(jnp.logical_and(inside, mine), entry, chosen)
        for t in range(per_patch):
            slot = me ^ (chosen * per_patch + t)
            slot_ref[s * per_patch + t : s * per_patch + t + 1, :] = jnp.full((1, slot_ref.shape[1]), slot)


def pack_kernel(heads, keys, both_ref, one_peer, two_peer, *refs):
    me = lax.axis_index("head")
    outs = refs[-len(keys) :]
    width = outs[0].shape[-1]
    for out, pairs in zip(outs, keys):
        for i, (u, w) in enumerate(pairs):
            one, two = (one_peer, two_peer) if u else (both_ref.at[0], both_ref.at[1])
            cols = pl.ds(pl.multiple_of((me ^ w) * width, width), width)
            out[i, 0], out[i, 1] = one[:, cols], two[:, cols]


def gather_kernel(places, *refs):
    for i, (a, j) in enumerate(places):
        refs[-1][i] = refs[a][j]


def pick_kernel(heads, places, slot_ref, *refs):
    arrays, outs = refs[:-2], refs[-2:]
    rows = arrays[0].shape[2]
    per_patch = outs[0].shape[1] // rows
    blocks = [arrays[a][j].astype(jnp.float32) for a, j in places]
    for s, out in enumerate(outs):
        for t in range(per_patch):
            slot = slot_ref[s * per_patch + t : s * per_patch + t + 1, :]
            value = blocks[0]
            for d in range(1, heads):
                value = jnp.where((slot == d)[None], blocks[d], value)
            out[:, t * rows : (t + 1) * rows, :] = value.astype(LOW)


def attend_kernel(heads, places, count, bias_ref, *refs):
    kv_arrays, qg_arrays, far, outs = refs[:count], refs[count : 2 * count], refs[2 * count : 2 * count + 2], refs[2 * count + 2 :]
    mq_kept, mq_sent, near_out, far_a, far_b, w_all, ds_all = outs
    kv = [kv_arrays[a].at[j] for a, j in places]
    qg = [qg_arrays[a].at[j] for a, j in places]
    rows, width = kv[0].shape[1:]
    patch = far[0].shape[1]
    queries = heads * rows
    groups = width // HEAD_DIM
    sizes = [rows] * heads + [patch, patch]
    bias = jnp.concatenate(
        [jnp.broadcast_to(bias_ref[b : b + 1, :], (n, queries)) for b, n in enumerate(sizes)], 0
    )
    keys = jnp.concatenate([r[0] for r in kv] + [r[0] for r in far], 0)
    values = jnp.concatenate([r[1] for r in kv] + [r[1] for r in far], 0)
    query = jnp.concatenate([r[0] for r in qg], 0)
    grad = jnp.concatenate([r[1] for r in qg], 0)
    keys_t, values_t = keys.T, values.T
    lane_head = lax.broadcasted_iota(jnp.int32, (1, width), 1) // HEAD_DIM
    scale = HEAD_DIM**-0.5
    mixed_t, qgrad_t, query_h, grad_h = [], [], [], []
    for head in range(groups):
        feats = slice(head * HEAD_DIM, (head + 1) * HEAD_DIM)
        lanes = slice(head * queries, (head + 1) * queries)
        query_h.append(jnp.where(lane_head == head, query, jnp.zeros_like(query)))
        grad_h.append(jnp.where(lane_head == head, grad, jnp.zeros_like(grad)))
        scores = dot(keys, query_h[head], NT) * (scale / math.log(2)) + bias
        weights = jnp.exp2(scores - jnp.max(scores, 0, keepdims=True))
        weights = weights * (1.0 / jnp.sum(weights, 0, keepdims=True))
        weights_low = weights.astype(LOW)
        grad_weights = dot(values, grad_h[head], NT)
        row_dots = jnp.sum(weights * grad_weights, 0, keepdims=True)
        grad_scores = (weights * (grad_weights - row_dots)).astype(LOW)
        w_all[:, lanes] = weights_low
        ds_all[:, lanes] = grad_scores
        mixed_t.append(dot(values_t[feats], weights_low))
        qgrad_t.append(dot(keys_t[feats], grad_scores) * scale)
    mixed = jnp.concatenate(mixed_t, 0).T.astype(LOW)
    qgrad = jnp.concatenate(qgrad_t, 0).T.astype(LOW)
    key_grad = dot(ds_all[...], jnp.concatenate(query_h, 0)) * scale
    value_grad = dot(w_all[...], jnp.concatenate(grad_h, 0))
    for d in range(heads):
        span = slice(d * rows, (d + 1) * rows)
        stay, go = split_at(heads, heads // 2)
        out = mq_kept.at[stay.index(d)] if d in stay else mq_sent.at[go.index(d)]
        out[0], out[1] = mixed[span], qgrad[span]
        near_out[d, 0], near_out[d, 1] = key_grad[span], value_grad[span]
    for s, out in enumerate((far_a, far_b)):
        span = slice(queries + s * patch, queries + (s + 1) * patch)
        out[0], out[1] = key_grad[span].astype(LOW), value_grad[span].astype(LOW)


def merge_kernel(heads, slot_ref, near, back_a, back_b, kept, sent):
    rows = near.shape[2]
    per_patch = back_a.shape[1] // rows
    for d in range(heads):
        total = near[d]
        for s, back in enumerate((back_a, back_b)):
            for t in range(per_patch):
                slot = slot_ref[s * per_patch + t : s * per_patch + t + 1, :]
                term = back[:, t * rows : (t + 1) * rows, :].astype(jnp.float32)
                total = total + jnp.where((slot == d)[None], term, 0.0)
        stay, go = split_at(heads, heads // 2)
        if d in stay:
            kept[stay.index(d)] = total.astype(LOW)
        else:
            sent[go.index(d)] = total.astype(LOW)


def unpack_kernel(heads, places, *refs):
    arrays, outs = refs[:-2], refs[-2:]
    width = arrays[0].shape[-1]
    me = lax.axis_index("head")
    for d, (a, j) in enumerate(places):
        cols = pl.ds(pl.multiple_of((me ^ d) * width, width), width)
        outs[0][:, cols], outs[1][:, cols] = arrays[a][j, 0], arrays[a][j, 1]


def swap(array, bit):
    heads = lax.axis_size("head")
    return lax.ppermute(array, "head", [(i, i ^ bit) for i in range(heads)])


def regroup(arrays, places):
    shape = jax.ShapeDtypeStruct((len(places),) + arrays[0].shape[1:], LOW)
    return call(functools.partial(gather_kernel, places), "regroup", [shape], *arrays)[0]


def exchange(bits, arrays, held, outgoing, going):
    for i, bit in enumerate(bits):
        if i:
            going = sorted(k for k in held if k[1] & bit)
            outgoing = regroup(arrays, [held.pop(k) for k in going])
        arrays.append(swap(outgoing, bit))
        for j, (u, w) in enumerate(going):
            held[(u + bit, w - bit)] = (len(arrays) - 1, j)
    return arrays, [held[(d, 0)] for d in range(lax.axis_size("head"))]


def gather_in(heads, one, two, block, *after):
    one_peer, two_peer = swap(one, 1), swap(two, 1)
    both = lax.optimization_barrier(jnp.concatenate([one, two], 0)).reshape((2,) + one.shape)
    keys = [[(u, w) for u in range(2) for w in range(0, heads, 2) if bool(w & 2) == b] for b in (False, True)]
    shapes = [jax.ShapeDtypeStruct((len(k),) + block, LOW) for k in keys]
    kept, sent = call(functools.partial(pack_kernel, heads, keys), "pack", shapes, both, one_peer, two_peer, *after)
    held = {k: (0, i) for i, k in enumerate(keys[0])}
    return exchange(all_bits(heads)[1:], [kept], held, sent, keys[1])


def scatter_out(heads, bits, kept, sent):
    stay, go = split_at(heads, bits[0])
    return exchange(bits, [kept], {(0, w): (0, i) for i, w in enumerate(stay)}, sent, [(0, w) for w in go])


def shards(queries, key_rows, value_rows, out_grads, neighbours):
    rows, features = queries.shape
    heads, owners = lax.axis_size("head"), lax.axis_size("node")
    width = features // heads
    local_count = neighbours.shape[0] // owners
    per_patch = heads // local_count
    patch = rows * per_patch
    half = jax.ShapeDtypeStruct((heads // 2, 2, rows, width), LOW)
    near_shape = jax.ShapeDtypeStruct((heads, 2, rows, width), jnp.float32)
    slab = jax.ShapeDtypeStruct((2, patch, width), LOW)
    whole = jax.ShapeDtypeStruct((rows, features), LOW)
    routes = pair_routes(owners, heads)
    span = heads * rows + 2 * patch
    lanes = width // HEAD_DIM * heads * rows

    kv, places = gather_in(heads, key_rows, value_rows, (2, rows, width))
    bias, slots = call(
        functools.partial(prep_kernel, heads, owners, local_count, per_patch, rows),
        "prep",
        [
            jax.ShapeDtypeStruct((heads + 2, heads * rows), jnp.float32),
            jax.ShapeDtypeStruct((2 * per_patch, width), jnp.int32),
        ],
        neighbours,
        kv[0],
        specs=[SMEM, VMEM],
    )
    qg, _ = gather_in(heads, queries, out_grads, (2, rows, width), slots)
    picked = call(functools.partial(pick_kernel, heads, places), "pick", [slab] * 2, slots, *kv)
    far = [lax.ppermute(p, ("node", "head"), r) for p, r in zip(picked, routes)]
    mq_kept, mq_sent, near, *far_grads = call(
        functools.partial(attend_kernel, heads, places, len(kv)),
        "attend",
        [half, half, near_shape, slab, slab],
        bias,
        *kv,
        *qg,
        *far,
        limit=24,
        scratch=[pltpu.VMEM((span, lanes), LOW)] * 2,
    )
    back = [lax.ppermute(p, ("node", "head"), r) for p, r in zip(far_grads, routes)]
    mq, mq_places = scatter_out(heads, all_bits(heads)[::-1], mq_kept, mq_sent)
    merged = call(functools.partial(merge_kernel, heads), "merge", [half] * 2, slots, near, *back)
    kv_grads, kv_places = scatter_out(heads, all_bits(heads)[::-1], *merged)
    unpack = functools.partial(unpack_kernel, heads)
    mixed, query_grad = call(functools.partial(unpack, mq_places), "unpack", [whole] * 2, *mq)
    key_grad, value_grad = call(functools.partial(unpack, kv_places), "unpack", [whole] * 2, *kv_grads)
    return mixed, query_grad, key_grad, value_grad


def solution(mesh):
    rows = P(("grp", "node", "head"), None)
    return jax.shard_map(
        shards,
        mesh=mesh,
        in_specs=(rows, rows, rows, rows, P("grp", None)),
        out_specs=(rows, rows, rows, rows),
        check_vma=False,
    )
```

```python
import functools
import math

import jax
import jax.numpy as jnp
from jax import lax
from jax.experimental import pallas as pl
from jax.experimental.pallas import tpu as pltpu
from jax.sharding import PartitionSpec as P

HEAD_DIM = 64
NEVER = -1e30
SCORE_SCALE = HEAD_DIM**-0.5 / math.log(2)
LOW = jnp.bfloat16
VMEM = pl.BlockSpec(memory_space=pltpu.VMEM)
SMEM = pl.BlockSpec(memory_space=pltpu.SMEM)
NT = (((1,), (1,)), ((), ()))


def dot(left, right, dims=(((1,), (0,)), ((), ()))):
    return lax.dot_general(left, right, dims, preferred_element_type=jnp.float32)


def call(kernel, name, outs, *args, limit=8, scratch=(), cost=None, specs=None):
    return pl.pallas_call(
        kernel,
        out_shape=outs,
        in_specs=specs or [VMEM] * len(args),
        out_specs=[VMEM] * len(outs),
        scratch_shapes=scratch,
        name=name,
        cost_estimate=cost,
        compiler_params=pltpu.CompilerParams(vmem_limit_bytes=limit * 1024 * 1024),
    )(*args)


def pair_routes(owners, heads):
    routes = []
    for step in (1, -1):
        route = []
        for n in range(owners):
            other = n + step * (1 - 2 * (n % 2))
            for h in range(heads):
                target = other * heads + h if 0 <= other < owners else n * heads + (h ^ 1)
                route.append((n * heads + h, target))
        routes.append(route)
    return routes


def prep_kernel(heads, owners, local_count, per_patch, rows, nbr_ref, after_ref, bias_ref, slot_ref):
    me, node = lax.axis_index("head"), lax.axis_index("node")
    odd = lax.rem(node, 2)
    pair = (node + 1 - 2 * odd, node - 1 + 2 * odd)
    queries = heads * rows
    own = [[jnp.int32(p == k) for k in range(local_count)] for p in range(local_count)]
    out_of = [[jnp.int32(0), jnp.int32(0)] for _ in range(local_count)]
    for p in range(local_count):
        for j in range(nbr_ref.shape[1]):
            entry = nbr_ref[node * local_count + p, j]
            for k in range(local_count):
                own[p][k] += jnp.where(entry == node * local_count + k, 1, 0)
            for s in range(2):
                start = pair[s] * local_count
                inside = jnp.logical_and(entry >= start, entry < start + local_count)
                out_of[p][s] += jnp.where(inside, 1, 0)

    def choose(index, values):
        value = values[0]
        for i in range(1, len(values)):
            value = jnp.where(index == i, values[i], value)
        return value

    patch_of = [(me ^ d) // per_patch for d in range(heads)]
    counts = [
        [choose(patch_of[e], [choose(patch_of[d], own[p]) for p in range(local_count)]) for e in range(heads)]
        for d in range(heads)
    ]
    for s in range(2):
        counts.append([choose(patch_of[e], [out_of[p][s] for p in range(local_count)]) for e in range(heads)])
    lane_block = lax.broadcasted_iota(jnp.int32, (1, queries), 1) // rows
    for b, row_counts in enumerate(counts):
        row = jnp.zeros((1, queries), jnp.float32)
        for e in range(heads):
            row = jnp.where(lane_block == e, row_counts[e].astype(jnp.float32), row)
        row = jnp.where(row > 0.5, jnp.log(jnp.maximum(row, 1.0)) * (1 / math.log(2)), NEVER)
        bias_ref[b : b + 1, :] = row
    for s in range(2):
        inside = jnp.logical_and(pair[s] >= 0, pair[s] < owners)
        first = jnp.where(inside, pair[s], 0) * local_count
        chosen = jnp.int32(0)
        for p in range(local_count):
            for j in range(nbr_ref.shape[1]):
                entry = nbr_ref[first + p, j] - node * local_count
                mine = jnp.logical_and(entry >= 0, entry < local_count)
                chosen = jnp.where(jnp.logical_and(inside, mine), entry, chosen)
        for t in range(per_patch):
            slot = me ^ (chosen * per_patch + t)
            slot_ref[s * per_patch + t : s * per_patch + t + 1, :] = jnp.full((1, slot_ref.shape[1]), slot)


def pack_kernel(heads, joint, *refs):
    one, two = (refs[0].at[0], refs[0].at[1]) if joint else refs[:2]
    me = lax.axis_index("head")
    width = refs[-1].shape[-1]
    for d, out in enumerate(refs[-heads:]):
        cols = pl.ds(pl.multiple_of((me ^ d) * width, width), width)
        out[0, 0], out[0, 1] = one[:, cols], two[:, cols]


def pick_kernel(heads, places, slot_ref, *refs):
    arrays, outs = refs[:-2], refs[-2:]
    rows = arrays[0].shape[2]
    per_patch = outs[0].shape[1] // rows
    blocks = [arrays[a][j].astype(jnp.float32) for a, j in places]
    for s, out in enumerate(outs):
        for t in range(per_patch):
            slot = slot_ref[s * per_patch + t : s * per_patch + t + 1, :]
            value = blocks[0]
            for d in range(1, heads):
                value = jnp.where((slot == d)[None], blocks[d], value)
            out[:, t * rows : (t + 1) * rows, :] = value.astype(LOW)


def masked(rows, groups):
    head_of = lax.broadcasted_iota(jnp.int32, (1, rows.shape[1]), 1) // HEAD_DIM
    return [jnp.where(head_of == head, rows, jnp.zeros_like(rows)) for head in range(groups)]


def spread(bias_ref, first, sizes):
    queries = bias_ref.shape[1]
    rows = [jnp.broadcast_to(bias_ref[first + i : first + i + 1, :], (n, queries)) for i, n in enumerate(sizes)]
    return jnp.concatenate(rows, 0)


def joined(arrays, places, which):
    return jnp.concatenate([arrays[a][j, which] for a, j in places], 0)


def near_kernel(heads, places, count, bias_ref, *refs):
    kv, qg, (exps_ref, gw_ref, stat_ref) = refs[:count], refs[count : 2 * count], refs[2 * count :]
    rows, width = kv[0].shape[2:]
    queries = heads * rows
    groups = width // HEAD_DIM
    bias = spread(bias_ref, 0, [rows] * heads)
    keys, values = joined(kv, places, 0), joined(kv, places, 1)
    query_h, grad_h = masked(joined(qg, places, 0), groups), masked(joined(qg, places, 1), groups)
    for head in range(groups):
        lanes = slice(head * queries, (head + 1) * queries)
        scores = dot(keys, query_h[head], NT) * SCORE_SCALE + bias
        top = jnp.max(scores, 0, keepdims=True)
        exps = jnp.exp2(scores - top)
        grad_weights = dot(values, grad_h[head], NT)
        exps_ref[:, lanes] = exps
        gw_ref[:, lanes] = grad_weights
        stat_ref[0:1, lanes] = top
        stat_ref[1:2, lanes] = jnp.sum(exps, 0, keepdims=True)
        stat_ref[2:3, lanes] = jnp.sum(exps * grad_weights, 0, keepdims=True)


def far_kernel(heads, places, count, bias_ref, stat_ref, *refs):
    qg, far, (w_ref, ds_ref, final_ref, far_a, far_b) = refs[:count], refs[count : count + 2], refs[count + 2 :]
    patch, width = far[0].shape[1:]
    queries = bias_ref.shape[1]
    groups = width // HEAD_DIM
    bias = spread(bias_ref, heads, [patch, patch])
    keys, values = jnp.concatenate([r[0] for r in far], 0), jnp.concatenate([r[1] for r in far], 0)
    query_h, grad_h = masked(joined(qg, places, 0), groups), masked(joined(qg, places, 1), groups)
    for head in range(groups):
        lanes = slice(head * queries, (head + 1) * queries)
        near_top = stat_ref[0:1, lanes]
        scores = dot(keys, query_h[head], NT) * SCORE_SCALE + bias
        top = jnp.maximum(near_top, jnp.max(scores, 0, keepdims=True))
        exps = jnp.exp2(scores - top)
        shrink = jnp.exp2(near_top - top)
        grad_weights = dot(values, grad_h[head], NT)
        part = 1.0 / (shrink * stat_ref[1:2, lanes] + jnp.sum(exps, 0, keepdims=True))
        weights = exps * part
        shrink = shrink * part
        row_dots = shrink * stat_ref[2:3, lanes] + jnp.sum(weights * grad_weights, 0, keepdims=True)
        w_ref[:, lanes] = weights.astype(LOW)
        ds_ref[:, lanes] = (weights * (grad_weights - row_dots)).astype(LOW)
        final_ref[0:1, lanes] = shrink
        final_ref[1:2, lanes] = row_dots
    key_grad = dot(ds_ref[...], jnp.concatenate(query_h, 0)) * HEAD_DIM**-0.5
    value_grad = dot(w_ref[...], jnp.concatenate(grad_h, 0))
    for s, out in enumerate((far_a, far_b)):
        span = slice(s * patch, (s + 1) * patch)
        out[0], out[1] = key_grad[span].astype(LOW), value_grad[span].astype(LOW)


def rest_kernel(heads, places, count, final_ref, exps_ref, gw_ref, far_w_ref, far_ds_ref, *refs):
    kv, qg, far = refs[:count], refs[count : 2 * count], refs[2 * count : 2 * count + 2]
    mq_out, (near_out, w_ref, ds_ref) = refs[2 * count + 2 : -3], refs[-3:]
    rows, width = kv[0].shape[2:]
    queries = heads * rows
    groups = width // HEAD_DIM
    scale = HEAD_DIM**-0.5
    keys_t, values_t = joined(kv, places, 0).T, joined(kv, places, 1).T
    far_keys_t = jnp.concatenate([r[0] for r in far], 0).T
    far_values_t = jnp.concatenate([r[1] for r in far], 0).T
    query_h, grad_h = masked(joined(qg, places, 0), groups), masked(joined(qg, places, 1), groups)
    mixed_t, qgrad_t = [], []
    for head in range(groups):
        feats = slice(head * HEAD_DIM, (head + 1) * HEAD_DIM)
        lanes = slice(head * queries, (head + 1) * queries)
        weights = exps_ref[:, lanes] * final_ref[0:1, lanes]
        low = weights.astype(LOW)
        grad_scores = (weights * (gw_ref[:, lanes] - final_ref[1:2, lanes])).astype(LOW)
        w_ref[:, lanes] = low
        ds_ref[:, lanes] = grad_scores
        mixed_t.append(dot(values_t[feats], low) + dot(far_values_t[feats], far_w_ref[:, lanes]))
        qgrad_t.append((dot(keys_t[feats], grad_scores) + dot(far_keys_t[feats], far_ds_ref[:, lanes])) * scale)
    mixed = jnp.concatenate(mixed_t, 0).T.astype(LOW)
    qgrad = jnp.concatenate(qgrad_t, 0).T.astype(LOW)
    key_grad = dot(ds_ref[...], jnp.concatenate(query_h, 0)) * scale
    value_grad = dot(w_ref[...], jnp.concatenate(grad_h, 0))
    for d in range(heads):
        span = slice(d * rows, (d + 1) * rows)
        mq_out[d][0, 0], mq_out[d][0, 1] = mixed[span], qgrad[span]
        near_out[d, 0], near_out[d, 1] = key_grad[span], value_grad[span]


def merge_kernel(heads, slot_ref, near, back_a, back_b, *outs):
    rows = near.shape[2]
    per_patch = back_a.shape[1] // rows
    for d in range(heads):
        total = near[d]
        for s, back in enumerate((back_a, back_b)):
            for t in range(per_patch):
                slot = slot_ref[s * per_patch + t : s * per_patch + t + 1, :]
                term = back[:, t * rows : (t + 1) * rows, :].astype(jnp.float32)
                total = total + jnp.where((slot == d)[None], term, 0.0)
        outs[d][0] = total.astype(LOW)


def unpack_kernel(heads, places, *refs):
    arrays, outs = refs[:-2], refs[-2:]
    width = arrays[0].shape[-1]
    me = lax.axis_index("head")
    for d, (a, j) in enumerate(places):
        cols = pl.ds(pl.multiple_of((me ^ d) * width, width), width)
        outs[0][:, cols], outs[1][:, cols] = arrays[a][j, 0], arrays[a][j, 1]


def exchange(blocks):
    heads = len(blocks)
    got = list(blocks)
    for d in sorted(range(1, heads), key=lambda d: (-(d >> 1), d)):
        got[d] = lax.ppermute(blocks[d], "head", [(i, i ^ d) for i in range(heads)])
    return got


def gather_in(heads, one, two, joint, block, *after):
    own = [one, two]
    if joint:
        own = [lax.optimization_barrier(jnp.concatenate(own, 0)).reshape((2,) + one.shape)]
    return exchange(call(functools.partial(pack_kernel, heads, joint), "pack", [block] * heads, *own, *after))


def shards(queries, key_rows, value_rows, out_grads, neighbours):
    rows, features = queries.shape
    heads, owners = lax.axis_size("head"), lax.axis_size("node")
    width = features // heads
    local_count = neighbours.shape[0] // owners
    per_patch = heads // local_count
    patch = rows * per_patch
    block = jax.ShapeDtypeStruct((1, 2, rows, width), LOW)
    places = [(d, 0) for d in range(heads)]
    near_shape = jax.ShapeDtypeStruct((heads, 2, rows, width), jnp.float32)
    slab = jax.ShapeDtypeStruct((2, patch, width), LOW)
    whole = jax.ShapeDtypeStruct((rows, features), LOW)
    routes = pair_routes(owners, heads)

    kv = gather_in(heads, key_rows, value_rows, True, block)
    bias, slots = call(
        functools.partial(prep_kernel, heads, owners, local_count, per_patch, rows),
        "prep",
        [
            jax.ShapeDtypeStruct((heads + 2, heads * rows), jnp.float32),
            jax.ShapeDtypeStruct((2 * per_patch, width), jnp.int32),
        ],
        neighbours,
        kv[0],
        specs=[SMEM, VMEM],
    )
    qg = gather_in(heads, queries, out_grads, False, block, slots)
    picked = call(functools.partial(pick_kernel, heads, places), "pick", [slab] * 2, slots, *kv)
    far = [lax.ppermute(p, ("node", "head"), r) for p, r in zip(picked, routes)]
    lanes = width // HEAD_DIM * heads * rows
    own, other = heads * rows, 2 * patch
    work = pl.CostEstimate(flops=1500000000, bytes_accessed=1, transcendentals=0)

    def table(height, kind=jnp.float32):
        return jax.ShapeDtypeStruct((height, lanes), kind)

    exps, grad_weights, stats = call(
        functools.partial(near_kernel, heads, places, len(kv)),
        "near",
        [table(own), table(own), table(3)],
        bias,
        *kv,
        *qg,
        cost=work,
    )
    far_w, far_ds, final, *far_grads = call(
        functools.partial(far_kernel, heads, places, len(kv)),
        "far",
        [table(other, LOW), table(other, LOW), table(2), slab, slab],
        bias,
        stats,
        *qg,
        *far,
        cost=work,
    )
    *mq, near = call(
        functools.partial(rest_kernel, heads, places, len(kv)),
        "rest",
        [block] * heads + [near_shape],
        final,
        exps,
        grad_weights,
        far_w,
        far_ds,
        *kv,
        *qg,
        *far,
        scratch=[pltpu.VMEM((own, lanes), LOW)] * 2,
        cost=work,
    )
    back = [lax.ppermute(p, ("node", "head"), r) for p, r in zip(far_grads, routes)]
    mq = exchange(mq)
    kv_grads = exchange(call(functools.partial(merge_kernel, heads), "merge", [block] * heads, slots, near, *back))
    unpack = functools.partial(unpack_kernel, heads, places)
    mixed, query_grad = call(unpack, "unpack", [whole] * 2, *mq)
    key_grad, value_grad = call(unpack, "unpack", [whole] * 2, *kv_grads)
    return mixed, query_grad, key_grad, value_grad


def solution(mesh):
    rows = P(("grp", "node", "head"), None)
    return jax.shard_map(
        shards,
        mesh=mesh,
        in_specs=(rows, rows, rows, rows, P("grp", None)),
        out_specs=(rows, rows, rows, rows),
        check_vma=False,
    )
```

```python
import functools
import math

import jax
import jax.numpy as jnp
from jax import lax
from jax.experimental import pallas as pl
from jax.experimental.pallas import tpu as pltpu
from jax.sharding import PartitionSpec as P

HEAD_DIM = 64
NEVER = -1e30
SCORE_SCALE = HEAD_DIM**-0.5 / math.log(2)
LOW = jnp.bfloat16
VMEM = pl.BlockSpec(memory_space=pltpu.VMEM)
SMEM = pl.BlockSpec(memory_space=pltpu.SMEM)


def dot(left, right):
    return jnp.dot(left, right, preferred_element_type=jnp.float32)


def call(kernel, name, outs, *args, limit=8, scratch=(), cost=None, specs=None):
    return pl.pallas_call(
        kernel,
        out_shape=outs,
        in_specs=specs or [VMEM] * len(args),
        out_specs=[VMEM] * len(outs),
        scratch_shapes=scratch,
        name=name,
        cost_estimate=cost,
        compiler_params=pltpu.CompilerParams(vmem_limit_bytes=limit * 1024 * 1024),
    )(*args)


def pair_routes(owners, heads):
    routes = []
    for step in (1, -1):
        route = []
        for n in range(owners):
            other = n + step * (1 - 2 * (n % 2))
            for h in range(heads):
                target = other * heads + h if 0 <= other < owners else n * heads + (h ^ 1)
                route.append((n * heads + h, target))
        routes.append(route)
    return routes


def prep_kernel(heads, owners, local_count, per_patch, rows, nbr_ref, after_ref, bias_ref, slot_ref):
    me, node = lax.axis_index("head"), lax.axis_index("node")
    odd = lax.rem(node, 2)
    pair = (node + 1 - 2 * odd, node - 1 + 2 * odd)
    queries = heads * rows
    own = [[jnp.int32(p == k) for k in range(local_count)] for p in range(local_count)]
    out_of = [[jnp.int32(0), jnp.int32(0)] for _ in range(local_count)]
    for p in range(local_count):
        for j in range(nbr_ref.shape[1]):
            entry = nbr_ref[node * local_count + p, j]
            for k in range(local_count):
                own[p][k] += jnp.where(entry == node * local_count + k, 1, 0)
            for s in range(2):
                start = pair[s] * local_count
                inside = jnp.logical_and(entry >= start, entry < start + local_count)
                out_of[p][s] += jnp.where(inside, 1, 0)

    def choose(index, values):
        value = values[0]
        for i in range(1, len(values)):
            value = jnp.where(index == i, values[i], value)
        return value

    patch_of = [(me ^ d) // per_patch for d in range(heads)]
    counts = [
        [choose(patch_of[e], [choose(patch_of[d], own[p]) for p in range(local_count)]) for e in range(heads)]
        for d in range(heads)
    ]
    for s in range(2):
        counts.append([choose(patch_of[e], [out_of[p][s] for p in range(local_count)]) for e in range(heads)])
    lane_block = lax.broadcasted_iota(jnp.int32, (1, queries), 1) // rows
    for b, row_counts in enumerate(counts):
        row = jnp.zeros((1, queries), jnp.float32)
        for e in range(heads):
            row = jnp.where(lane_block == e, row_counts[e].astype(jnp.float32), row)
        row = jnp.where(row > 0.5, jnp.log(jnp.maximum(row, 1.0)) * (1 / math.log(2)), NEVER)
        bias_ref[b : b + 1, :] = row
    for s in range(2):
        inside = jnp.logical_and(pair[s] >= 0, pair[s] < owners)
        first = jnp.where(inside, pair[s], 0) * local_count
        chosen = jnp.int32(0)
        for p in range(local_count):
            for j in range(nbr_ref.shape[1]):
                entry = nbr_ref[first + p, j] - node * local_count
                mine = jnp.logical_and(entry >= 0, entry < local_count)
                chosen = jnp.where(jnp.logical_and(inside, mine), entry, chosen)
        for t in range(per_patch):
            slot = me ^ (chosen * per_patch + t)
            slot_ref[s * per_patch + t : s * per_patch + t + 1, :] = jnp.full((1, slot_ref.shape[1]), slot)


def pack_kernel(heads, joint, *refs):
    one, two = (refs[0].at[0], refs[0].at[1]) if joint else refs[:2]
    me = lax.axis_index("head")
    width = refs[-1].shape[-1]
    for d, out in enumerate(refs[-heads:]):
        cols = pl.ds(pl.multiple_of((me ^ d) * width, width), width)
        out[0, 0], out[0, 1] = one[:, cols], two[:, cols]


def pick_kernel(heads, places, slot_ref, *refs):
    arrays, outs = refs[:-2], refs[-2:]
    rows = arrays[0].shape[2]
    per_patch = outs[0].shape[1] // rows
    blocks = [arrays[a][j].astype(jnp.float32) for a, j in places]
    for s, out in enumerate(outs):
        for t in range(per_patch):
            slot = slot_ref[s * per_patch + t : s * per_patch + t + 1, :]
            value = blocks[0]
            for d in range(1, heads):
                value = jnp.where((slot == d)[None], blocks[d], value)
            out[:, t * rows : (t + 1) * rows, :] = value.astype(LOW)


def spread(bias_ref, first, sizes):
    queries = bias_ref.shape[1]
    rows = [jnp.broadcast_to(bias_ref[first + i : first + i + 1, :], (n, queries)) for i, n in enumerate(sizes)]
    return jnp.concatenate(rows, 0)


def joined(arrays, places, which):
    return jnp.concatenate([arrays[a][j, which] for a, j in places], 0)


def near_kernel(heads, places, count, bias_ref, *refs):
    kv, qg, outs = refs[:count], refs[count : 2 * count], refs[2 * count :]
    exps_ref, gw_ref, stat_ref, *sides = outs
    rows, width = kv[0].shape[2:]
    queries = heads * rows
    groups = width // HEAD_DIM
    bias = spread(bias_ref, 0, [rows] * heads)
    keys, values = joined(kv, places, 0), joined(kv, places, 1)
    lane_head = lax.broadcasted_iota(jnp.int32, (1, width), 1) // HEAD_DIM
    for which, (down, across) in enumerate((sides[:2], sides[2:])):
        whole = joined(qg, places, which)
        turned = whole.T
        across[...] = jnp.zeros_like(across)
        for head in range(groups):
            feats = slice(head * HEAD_DIM, (head + 1) * HEAD_DIM)
            lanes = slice(head * queries, (head + 1) * queries)
            down[lanes, :] = jnp.where(lane_head == head, whole, jnp.zeros_like(whole))
            across[feats, lanes] = turned[feats]
    for head in range(groups):
        lanes = slice(head * queries, (head + 1) * queries)
        scores = dot(keys, sides[1][:, lanes]) * SCORE_SCALE + bias
        top = jnp.max(scores, 0, keepdims=True)
        exps = jnp.exp2(scores - top)
        grad_weights = dot(values, sides[3][:, lanes])
        exps_ref[:, lanes] = exps
        gw_ref[:, lanes] = grad_weights
        stat_ref[0:1, lanes] = top
        stat_ref[1:2, lanes] = jnp.sum(exps, 0, keepdims=True)
        stat_ref[2:3, lanes] = jnp.sum(exps * grad_weights, 0, keepdims=True)


def first_kernel(heads, bias_ref, query_across, grad_across, keys_ref, exps_ref, gw_ref, stat_ref):
    queries = bias_ref.shape[1]
    patch, width = keys_ref.shape[1:]
    bias = spread(bias_ref, heads, [patch])
    for head in range(width // HEAD_DIM):
        lanes = slice(head * queries, (head + 1) * queries)
        scores = dot(keys_ref[0], query_across[:, lanes]) * SCORE_SCALE + bias
        top = jnp.max(scores, 0, keepdims=True)
        exps = jnp.where(bias > NEVER, jnp.exp2(scores - top), 0.0)
        grad_weights = dot(keys_ref[1], grad_across[:, lanes])
        exps_ref[:, lanes] = exps
        gw_ref[:, lanes] = grad_weights
        stat_ref[0:1, lanes] = top
        stat_ref[1:2, lanes] = jnp.sum(exps, 0, keepdims=True)
        stat_ref[2:3, lanes] = jnp.sum(exps * grad_weights, 0, keepdims=True)


def far_kernel(heads, bias_ref, stat_ref, exps_ref, gw_ref, first_ref, query_down, query_across, grad_down, *refs):
    grad_across, second_ref, w_ref, ds_ref, final_ref, far_a, far_b = refs
    patch, width = second_ref.shape[1:]
    queries = bias_ref.shape[1]
    bias = spread(bias_ref, heads + 1, [patch])
    for head in range(width // HEAD_DIM):
        lanes = slice(head * queries, (head + 1) * queries)
        near_top, first_top = stat_ref[0:1, lanes], first_ref[0:1, lanes]
        scores = dot(second_ref[0], query_across[:, lanes]) * SCORE_SCALE + bias
        top = jnp.maximum(jnp.maximum(near_top, first_top), jnp.max(scores, 0, keepdims=True))
        exps = jnp.exp2(scores - top)
        shrink, first_shrink = jnp.exp2(near_top - top), jnp.exp2(first_top - top)
        grad_weights = dot(second_ref[1], grad_across[:, lanes])
        total = shrink * stat_ref[1:2, lanes] + first_shrink * first_ref[1:2, lanes]
        part = 1.0 / (total + jnp.sum(exps, 0, keepdims=True))
        weights = exps * part
        shrink, first_shrink = shrink * part, first_shrink * part
        row_dots = shrink * stat_ref[2:3, lanes] + first_shrink * first_ref[2:3, lanes]
        row_dots = row_dots + jnp.sum(weights * grad_weights, 0, keepdims=True)
        w_ref[patch:, lanes] = weights.astype(LOW)
        ds_ref[patch:, lanes] = (weights * (grad_weights - row_dots)).astype(LOW)
        weights = exps_ref[:, lanes] * first_shrink
        w_ref[:patch, lanes] = weights.astype(LOW)
        ds_ref[:patch, lanes] = (weights * (gw_ref[:, lanes] - row_dots)).astype(LOW)
        final_ref[0:1, lanes] = shrink
        final_ref[1:2, lanes] = row_dots
    key_grad = dot(ds_ref[...], query_down[...]) * HEAD_DIM**-0.5
    value_grad = dot(w_ref[...], grad_down[...])
    for s, out in enumerate((far_a, far_b)):
        span = slice(s * patch, (s + 1) * patch)
        out[0], out[1] = key_grad[span].astype(LOW), value_grad[span].astype(LOW)


def rest_kernel(heads, places, final_ref, exps_ref, gw_ref, far_w_ref, far_ds_ref, query_down, grad_down, *refs):
    kv, far, outs = refs[:heads], refs[heads : heads + 2], refs[heads + 2 : -3]
    near_out, w_ref, ds_ref = refs[-3:]
    rows, width = kv[0].shape[2:]
    queries = heads * rows
    keys_t, values_t = joined(kv, places, 0).T, joined(kv, places, 1).T
    far_keys_t = jnp.concatenate([r[0] for r in far], 0).T
    far_values_t = jnp.concatenate([r[1] for r in far], 0).T
    mixed_t, qgrad_t = [], []
    for head in range(width // HEAD_DIM):
        feats = slice(head * HEAD_DIM, (head + 1) * HEAD_DIM)
        lanes = slice(head * queries, (head + 1) * queries)
        weights = exps_ref[:, lanes] * final_ref[0:1, lanes]
        low = weights.astype(LOW)
        grad_scores = (weights * (gw_ref[:, lanes] - final_ref[1:2, lanes])).astype(LOW)
        w_ref[:, lanes] = low
        ds_ref[:, lanes] = grad_scores
        mixed_t.append(dot(values_t[feats], low) + dot(far_values_t[feats], far_w_ref[:, lanes]))
        qgrad_t.append((dot(keys_t[feats], grad_scores) + dot(far_keys_t[feats], far_ds_ref[:, lanes])) * HEAD_DIM**-0.5)
    mixed = jnp.concatenate(mixed_t, 0).T.astype(LOW)
    qgrad = jnp.concatenate(qgrad_t, 0).T.astype(LOW)
    key_grad = dot(ds_ref[...], query_down[...]) * HEAD_DIM**-0.5
    value_grad = dot(w_ref[...], grad_down[...])
    for d, out in enumerate(outs):
        span = slice(d * rows, (d + 1) * rows)
        out[0, 0], out[0, 1] = mixed[span], qgrad[span]
        near_out[d, 0], near_out[d, 1] = key_grad[span], value_grad[span]


def merge_kernel(heads, slot_ref, near, back_a, back_b, *outs):
    rows = near.shape[2]
    per_patch = back_a.shape[1] // rows
    me = lax.axis_index("head")
    for d in range(heads):
        total = near[d]
        part = lax.rem(me ^ d, per_patch)
        for s, back in enumerate((back_a, back_b)):
            slot = slot_ref[pl.ds(s * per_patch + part, 1), :]
            term = back[:, pl.ds(pl.multiple_of(part * rows, rows), rows), :].astype(jnp.float32)
            total = total + jnp.where((slot == d)[None], term, 0.0)
        outs[d][0] = total.astype(LOW)


def unpack_kernel(heads, places, *refs):
    arrays, outs = refs[:-2], refs[-2:]
    width = arrays[0].shape[-1]
    me = lax.axis_index("head")
    for d, (a, j) in enumerate(places):
        cols = pl.ds(pl.multiple_of((me ^ d) * width, width), width)
        outs[0][:, cols], outs[1][:, cols] = arrays[a][j, 0], arrays[a][j, 1]


def far_first(heads):
    return [0] + sorted(range(1, heads), key=lambda d: (-(d >> 1), d))


def exchange(blocks):
    heads = len(blocks)
    swaps = [[(i, i ^ d) for i in range(heads)] for d in range(heads)]
    return [lax.ppermute(blocks[d], "head", swaps[d]) if d else blocks[0] for d in far_first(heads)]


def gather_in(heads, one, two, joint, block, *after):
    own = [one, two]
    if joint:
        own = [lax.optimization_barrier(jnp.concatenate(own, 0)).reshape((2,) + one.shape)]
    return exchange(call(functools.partial(pack_kernel, heads, joint), "pack", [block] * heads, *own, *after))


def shards(queries, key_rows, value_rows, out_grads, neighbours):
    rows, features = queries.shape
    heads, owners = lax.axis_size("head"), lax.axis_size("node")
    width = features // heads
    local_count = neighbours.shape[0] // owners
    per_patch = heads // local_count
    patch = rows * per_patch
    block = jax.ShapeDtypeStruct((1, 2, rows, width), LOW)
    places = [(far_first(heads).index(d), 0) for d in range(heads)]
    near_shape = jax.ShapeDtypeStruct((heads, 2, rows, width), jnp.float32)
    slab = jax.ShapeDtypeStruct((2, patch, width), LOW)
    whole = jax.ShapeDtypeStruct((rows, features), LOW)
    routes = pair_routes(owners, heads)

    kv = gather_in(heads, key_rows, value_rows, True, block)
    bias, slots = call(
        functools.partial(prep_kernel, heads, owners, local_count, per_patch, rows),
        "prep",
        [
            jax.ShapeDtypeStruct((heads + 2, heads * rows), jnp.float32),
            jax.ShapeDtypeStruct((2 * per_patch, width), jnp.int32),
        ],
        neighbours,
        kv[0],
        specs=[SMEM, VMEM],
    )
    qg = gather_in(heads, queries, out_grads, False, block, slots)
    picked = call(functools.partial(pick_kernel, heads, places), "pick", [slab] * 2, slots, *kv)
    far = [lax.ppermute(p, ("node", "head"), r) for p, r in zip(picked, routes)]
    lanes = width // HEAD_DIM * heads * rows
    own, other = heads * rows, 2 * patch
    work = pl.CostEstimate(flops=1500000000, bytes_accessed=1, transcendentals=0)

    def table(height, kind=jnp.float32):
        return jax.ShapeDtypeStruct((height, lanes), kind)

    down = jax.ShapeDtypeStruct((lanes, width), LOW)
    across = jax.ShapeDtypeStruct((width, lanes), LOW)
    exps, grad_weights, stats, *sides = call(
        functools.partial(near_kernel, heads, places, len(kv)),
        "near",
        [table(own), table(own), table(3), down, across, down, across],
        bias,
        *kv,
        *qg,
        cost=work,
    )
    first = call(
        functools.partial(first_kernel, heads),
        "first",
        [table(patch), table(patch), table(3)],
        bias,
        sides[1],
        sides[3],
        far[0],
    )
    far_w, far_ds, final, *far_grads = call(
        functools.partial(far_kernel, heads),
        "far",
        [table(other, LOW), table(other, LOW), table(2), slab, slab],
        bias,
        stats,
        *first,
        *sides,
        far[1],
        cost=work,
    )
    *mq, near = call(
        functools.partial(rest_kernel, heads, places),
        "rest",
        [block] * heads + [near_shape],
        final,
        exps,
        grad_weights,
        far_w,
        far_ds,
        sides[0],
        sides[2],
        *kv,
        *far,
        scratch=[pltpu.VMEM((own, lanes), LOW)] * 2,
        cost=work,
    )
    back = [lax.ppermute(p, ("node", "head"), r) for p, r in zip(far_grads, routes)]
    mq = exchange(mq)
    kv_grads = exchange(call(functools.partial(merge_kernel, heads), "merge", [block] * heads, slots, near, *back))
    unpack = functools.partial(unpack_kernel, heads, places)
    mixed, query_grad = call(unpack, "unpack", [whole] * 2, *mq)
    key_grad, value_grad = call(unpack, "unpack", [whole] * 2, *kv_grads)
    return mixed, query_grad, key_grad, value_grad


def solution(mesh):
    rows = P(("grp", "node", "head"), None)
    return jax.shard_map(
        shards,
        mesh=mesh,
        in_specs=(rows, rows, rows, rows, P("grp", None)),
        out_specs=(rows, rows, rows, rows),
        check_vma=False,
    )
```

```python
import functools
import math

import jax
import jax.numpy as jnp
from jax import lax
from jax.experimental import pallas as pl
from jax.experimental.pallas import tpu as pltpu
from jax.sharding import PartitionSpec as P

HEAD_DIM = 64
NEVER = -1e30
SCORE_SCALE = HEAD_DIM**-0.5 / math.log(2)
LOW = jnp.bfloat16
VMEM = pl.BlockSpec(memory_space=pltpu.VMEM)
SMEM = pl.BlockSpec(memory_space=pltpu.SMEM)


def dot(left, right):
    return jnp.dot(left, right, preferred_element_type=jnp.float32)


def call(kernel, name, outs, *args, limit=8, scratch=(), cost=None, specs=None):
    return pl.pallas_call(
        kernel,
        out_shape=outs,
        in_specs=specs or [VMEM] * len(args),
        out_specs=[VMEM] * len(outs),
        scratch_shapes=scratch,
        name=name,
        cost_estimate=cost,
        compiler_params=pltpu.CompilerParams(vmem_limit_bytes=limit * 1024 * 1024),
    )(*args)


def pair_routes(owners, heads):
    routes = []
    for step in (1, -1):
        route = []
        for n in range(owners):
            other = n + step * (1 - 2 * (n % 2))
            for h in range(heads):
                target = other * heads + h if 0 <= other < owners else n * heads + (h ^ 1)
                route.append((n * heads + h, target))
        routes.append(route)
    return routes


def prep_kernel(heads, owners, local_count, per_patch, rows, nbr_ref, after_ref, bias_ref, slot_ref):
    me, node = lax.axis_index("head"), lax.axis_index("node")
    odd = lax.rem(node, 2)
    pair = (node + 1 - 2 * odd, node - 1 + 2 * odd)
    queries = heads * rows
    own = [[jnp.int32(p == k) for k in range(local_count)] for p in range(local_count)]
    out_of = [[jnp.int32(0), jnp.int32(0)] for _ in range(local_count)]
    for p in range(local_count):
        for j in range(nbr_ref.shape[1]):
            entry = nbr_ref[node * local_count + p, j]
            for k in range(local_count):
                own[p][k] += jnp.where(entry == node * local_count + k, 1, 0)
            for s in range(2):
                start = pair[s] * local_count
                inside = jnp.logical_and(entry >= start, entry < start + local_count)
                out_of[p][s] += jnp.where(inside, 1, 0)

    def choose(index, values):
        value = values[0]
        for i in range(1, len(values)):
            value = jnp.where(index == i, values[i], value)
        return value

    patch_of = [(me ^ d) // per_patch for d in range(heads)]
    counts = [
        [choose(patch_of[e], [choose(patch_of[d], own[p]) for p in range(local_count)]) for e in range(heads)]
        for d in range(heads)
    ]
    for s in range(2):
        counts.append([choose(patch_of[e], [out_of[p][s] for p in range(local_count)]) for e in range(heads)])
    lane_block = lax.broadcasted_iota(jnp.int32, (1, queries), 1) // rows
    for b, row_counts in enumerate(counts):
        row = jnp.zeros((1, queries), jnp.float32)
        for e in range(heads):
            row = jnp.where(lane_block == e, row_counts[e].astype(jnp.float32), row)
        row = jnp.where(row > 0.5, jnp.log(jnp.maximum(row, 1.0)) * (1 / math.log(2)), NEVER)
        bias_ref[b : b + 1, :] = row
    for s in range(2):
        inside = jnp.logical_and(pair[s] >= 0, pair[s] < owners)
        first = jnp.where(inside, pair[s], 0) * local_count
        chosen = jnp.int32(0)
        for p in range(local_count):
            for j in range(nbr_ref.shape[1]):
                entry = nbr_ref[first + p, j] - node * local_count
                mine = jnp.logical_and(entry >= 0, entry < local_count)
                chosen = jnp.where(jnp.logical_and(inside, mine), entry, chosen)
        for t in range(per_patch):
            slot = me ^ (chosen * per_patch + t)
            slot_ref[s * per_patch + t : s * per_patch + t + 1, :] = jnp.full((1, slot_ref.shape[1]), slot)


def pack_kernel(heads, one, two, *refs):
    me = lax.axis_index("head")
    width = refs[-1].shape[-1]
    for d, out in enumerate(refs[-heads:]):
        cols = pl.ds(pl.multiple_of((me ^ d) * width, width), width)
        out[0, 0], out[0, 1] = one[:, cols], two[:, cols]


def pick_kernel(heads, places, slot_ref, *refs):
    arrays, outs = refs[:-2], refs[-2:]
    rows = arrays[0].shape[2]
    per_patch = outs[0].shape[1] // rows
    blocks = [arrays[a][j].astype(jnp.float32) for a, j in places]
    for s, out in enumerate(outs):
        for t in range(per_patch):
            slot = slot_ref[s * per_patch + t : s * per_patch + t + 1, :]
            value = blocks[0]
            for d in range(1, heads):
                value = jnp.where((slot == d)[None], blocks[d], value)
            out[:, t * rows : (t + 1) * rows, :] = value.astype(LOW)


def spread(bias_ref, first, sizes):
    queries = bias_ref.shape[1]
    rows = [jnp.broadcast_to(bias_ref[first + i : first + i + 1, :], (n, queries)) for i, n in enumerate(sizes)]
    return jnp.concatenate(rows, 0)


def joined(arrays, places, which):
    return jnp.concatenate([arrays[a][j, which] for a, j in places], 0)


def near_kernel(heads, places, count, bias_ref, *refs):
    kv, qg, outs = refs[:count], refs[count : 2 * count], refs[2 * count :]
    exps_ref, gw_ref, stat_ref, *sides = outs
    rows, width = kv[0].shape[2:]
    queries = heads * rows
    groups = width // HEAD_DIM
    bias = spread(bias_ref, 0, [rows] * heads)
    keys, values = joined(kv, places, 0), joined(kv, places, 1)
    lane_head = lax.broadcasted_iota(jnp.int32, (1, width), 1) // HEAD_DIM
    for which, (down, across) in enumerate((sides[:2], sides[2:])):
        whole = joined(qg, places, which)
        turned = whole.T
        across[...] = jnp.zeros_like(across)
        for head in range(groups):
            feats = slice(head * HEAD_DIM, (head + 1) * HEAD_DIM)
            lanes = slice(head * queries, (head + 1) * queries)
            down[lanes, :] = jnp.where(lane_head == head, whole, jnp.zeros_like(whole))
            across[feats, lanes] = turned[feats]
    for head in range(groups):
        lanes = slice(head * queries, (head + 1) * queries)
        scores = dot(keys, sides[1][:, lanes]) * SCORE_SCALE + bias
        top = jnp.max(scores, 0, keepdims=True)
        exps = jnp.exp2(scores - top)
        grad_weights = dot(values, sides[3][:, lanes])
        exps_ref[:, lanes] = exps
        gw_ref[:, lanes] = grad_weights
        stat_ref[0:1, lanes] = top
        stat_ref[1:2, lanes] = jnp.sum(exps, 0, keepdims=True)
        stat_ref[2:3, lanes] = jnp.sum(exps * grad_weights, 0, keepdims=True)


def first_kernel(heads, bias_ref, query_across, grad_across, keys_ref, exps_ref, gw_ref, stat_ref):
    queries = bias_ref.shape[1]
    patch, width = keys_ref.shape[1:]
    bias = spread(bias_ref, heads, [patch])
    for head in range(width // HEAD_DIM):
        lanes = slice(head * queries, (head + 1) * queries)
        scores = dot(keys_ref[0], query_across[:, lanes]) * SCORE_SCALE + bias
        top = jnp.max(scores, 0, keepdims=True)
        exps = jnp.where(bias > NEVER, jnp.exp2(scores - top), 0.0)
        grad_weights = dot(keys_ref[1], grad_across[:, lanes])
        exps_ref[:, lanes] = exps
        gw_ref[:, lanes] = grad_weights
        stat_ref[0:1, lanes] = top
        stat_ref[1:2, lanes] = jnp.sum(exps, 0, keepdims=True)
        stat_ref[2:3, lanes] = jnp.sum(exps * grad_weights, 0, keepdims=True)


def far_kernel(heads, bias_ref, stat_ref, exps_ref, gw_ref, first_ref, query_down, query_across, grad_down, *refs):
    grad_across, second_ref, w_ref, ds_ref, final_ref, far_a, far_b = refs
    patch, width = second_ref.shape[1:]
    queries = bias_ref.shape[1]
    bias = spread(bias_ref, heads + 1, [patch])
    for head in range(width // HEAD_DIM):
        lanes = slice(head * queries, (head + 1) * queries)
        near_top, first_top = stat_ref[0:1, lanes], first_ref[0:1, lanes]
        scores = dot(second_ref[0], query_across[:, lanes]) * SCORE_SCALE + bias
        top = jnp.maximum(jnp.maximum(near_top, first_top), jnp.max(scores, 0, keepdims=True))
        exps = jnp.exp2(scores - top)
        shrink, first_shrink = jnp.exp2(near_top - top), jnp.exp2(first_top - top)
        grad_weights = dot(second_ref[1], grad_across[:, lanes])
        total = shrink * stat_ref[1:2, lanes] + first_shrink * first_ref[1:2, lanes]
        part = 1.0 / (total + jnp.sum(exps, 0, keepdims=True))
        weights = exps * part
        shrink, first_shrink = shrink * part, first_shrink * part
        row_dots = shrink * stat_ref[2:3, lanes] + first_shrink * first_ref[2:3, lanes]
        row_dots = row_dots + jnp.sum(weights * grad_weights, 0, keepdims=True)
        w_ref[patch:, lanes] = weights.astype(LOW)
        ds_ref[patch:, lanes] = (weights * (grad_weights - row_dots)).astype(LOW)
        weights = exps_ref[:, lanes] * first_shrink
        w_ref[:patch, lanes] = weights.astype(LOW)
        ds_ref[:patch, lanes] = (weights * (gw_ref[:, lanes] - row_dots)).astype(LOW)
        final_ref[0:1, lanes] = shrink
        final_ref[1:2, lanes] = row_dots
    key_grad = dot(ds_ref[...], query_down[...]) * HEAD_DIM**-0.5
    value_grad = dot(w_ref[...], grad_down[...])
    for s, out in enumerate((far_a, far_b)):
        span = slice(s * patch, (s + 1) * patch)
        out[0], out[1] = key_grad[span].astype(LOW), value_grad[span].astype(LOW)


def rest_kernel(heads, places, final_ref, exps_ref, gw_ref, far_w_ref, far_ds_ref, query_down, grad_down, *refs):
    kv, far, outs = refs[:heads], refs[heads : heads + 2], refs[heads + 2 : -3]
    near_out, w_ref, ds_ref = refs[-3:]
    rows, width = kv[0].shape[2:]
    queries = heads * rows
    keys_t, values_t = joined(kv, places, 0).T, joined(kv, places, 1).T
    far_keys_t = jnp.concatenate([r[0] for r in far], 0).T
    far_values_t = jnp.concatenate([r[1] for r in far], 0).T
    mixed_t, qgrad_t = [], []
    for head in range(width // HEAD_DIM):
        feats = slice(head * HEAD_DIM, (head + 1) * HEAD_DIM)
        lanes = slice(head * queries, (head + 1) * queries)
        weights = exps_ref[:, lanes] * final_ref[0:1, lanes]
        low = weights.astype(LOW)
        grad_scores = (weights * (gw_ref[:, lanes] - final_ref[1:2, lanes])).astype(LOW)
        w_ref[:, lanes] = low
        ds_ref[:, lanes] = grad_scores
        mixed_t.append(dot(values_t[feats], low) + dot(far_values_t[feats], far_w_ref[:, lanes]))
        qgrad_t.append((dot(keys_t[feats], grad_scores) + dot(far_keys_t[feats], far_ds_ref[:, lanes])) * HEAD_DIM**-0.5)
    mixed = jnp.concatenate(mixed_t, 0).T.astype(LOW)
    qgrad = jnp.concatenate(qgrad_t, 0).T.astype(LOW)
    key_grad = dot(ds_ref[...], query_down[...]) * HEAD_DIM**-0.5
    value_grad = dot(w_ref[...], grad_down[...])
    for d, out in enumerate(outs):
        span = slice(d * rows, (d + 1) * rows)
        out[0, 0], out[0, 1] = mixed[span], qgrad[span]
        near_out[d, 0], near_out[d, 1] = key_grad[span], value_grad[span]


def merge_kernel(heads, slot_ref, near, back_a, back_b, *outs):
    rows = near.shape[2]
    per_patch = back_a.shape[1] // rows
    me = lax.axis_index("head")
    for d in range(heads):
        total = near[d]
        part = lax.rem(me ^ d, per_patch)
        for s, back in enumerate((back_a, back_b)):
            slot = slot_ref[pl.ds(s * per_patch + part, 1), :]
            term = back[:, pl.ds(pl.multiple_of(part * rows, rows), rows), :].astype(jnp.float32)
            total = total + jnp.where((slot == d)[None], term, 0.0)
        outs[d][0] = total.astype(LOW)


def join_kernel(*refs):
    count = len(refs) // 3
    for i, out in enumerate(refs[2 * count :]):
        out[0, 0], out[0, 1] = refs[2 * i][...], refs[2 * i + 1][...]


def unpack_kernel(heads, places, *refs):
    arrays, outs = refs[:-2], refs[-2:]
    width = arrays[0].shape[-1]
    me = lax.axis_index("head")
    for d, (a, j) in enumerate(places):
        cols = pl.ds(pl.multiple_of((me ^ d) * width, width), width)
        outs[0][:, cols], outs[1][:, cols] = arrays[a][j, 0], arrays[a][j, 1]


def far_first(heads):
    return [0] + sorted(range(1, heads), key=lambda d: (-(d >> 1), d))


def exchange(blocks, order):
    heads = len(blocks)
    swaps = [[(i, i ^ d) for i in range(heads)] for d in range(heads)]
    return [lax.ppermute(blocks[d], "head", swaps[d]) if d else blocks[0] for d in order]


def cut(one, two, heads):
    me = lax.axis_index("head")
    width = one.shape[1] // heads
    starts = [(me ^ d) * width for d in range(heads)]
    parts = [[lax.dynamic_slice_in_dim(a, at, width, 1) for a in (one, two)] for at in starts]
    return call(join_kernel, "join", [jax.ShapeDtypeStruct((1, 2) + parts[0][0].shape, LOW)] * heads, *sum(parts, []))


def shards(queries, key_rows, value_rows, out_grads, neighbours):
    rows, features = queries.shape
    heads, owners = lax.axis_size("head"), lax.axis_size("node")
    width = features // heads
    local_count = neighbours.shape[0] // owners
    per_patch = heads // local_count
    patch = rows * per_patch
    block = jax.ShapeDtypeStruct((1, 2, rows, width), LOW)
    order, downward = far_first(heads), [0] + list(range(heads - 1, 0, -1))
    places = [(order.index(d), 0) for d in range(heads)]
    near_shape = jax.ShapeDtypeStruct((heads, 2, rows, width), jnp.float32)
    slab = jax.ShapeDtypeStruct((2, patch, width), LOW)
    whole = jax.ShapeDtypeStruct((rows, features), LOW)
    routes = pair_routes(owners, heads)

    kv = exchange(cut(key_rows, value_rows, heads), order)
    bias, slots = call(
        functools.partial(prep_kernel, heads, owners, local_count, per_patch, rows),
        "prep",
        [
            jax.ShapeDtypeStruct((heads + 2, heads * rows), jnp.float32),
            jax.ShapeDtypeStruct((2 * per_patch, width), jnp.int32),
        ],
        neighbours,
        kv[0],
        specs=[SMEM, VMEM],
    )
    pack = functools.partial(pack_kernel, heads)
    qg = exchange(call(pack, "pack", [block] * heads, queries, out_grads, slots), order)
    picked = call(functools.partial(pick_kernel, heads, places), "pick", [slab] * 2, slots, *kv)
    far = [lax.ppermute(p, ("node", "head"), r) for p, r in zip(picked, routes)]
    lanes = width // HEAD_DIM * heads * rows
    own, other = heads * rows, 2 * patch
    work = pl.CostEstimate(flops=1500000000, bytes_accessed=1, transcendentals=0)

    def table(height, kind=jnp.float32):
        return jax.ShapeDtypeStruct((height, lanes), kind)

    down = jax.ShapeDtypeStruct((lanes, width), LOW)
    across = jax.ShapeDtypeStruct((width, lanes), LOW)
    exps, grad_weights, stats, *sides = call(
        functools.partial(near_kernel, heads, places, len(kv)),
        "near",
        [table(own), table(own), table(3), down, across, down, across],
        bias,
        *kv,
        *qg,
        cost=work,
    )
    first = call(
        functools.partial(first_kernel, heads),
        "first",
        [table(patch), table(patch), table(3)],
        bias,
        sides[1],
        sides[3],
        far[0],
    )
    far_w, far_ds, final, *far_grads = call(
        functools.partial(far_kernel, heads),
        "far",
        [table(other, LOW), table(other, LOW), table(2), slab, slab],
        bias,
        stats,
        *first,
        *sides,
        far[1],
        cost=work,
    )
    *mq, near = call(
        functools.partial(rest_kernel, heads, places),
        "rest",
        [block] * heads + [near_shape],
        final,
        exps,
        grad_weights,
        far_w,
        far_ds,
        sides[0],
        sides[2],
        *kv,
        *far,
        scratch=[pltpu.VMEM((own, lanes), LOW)] * 2,
        cost=work,
    )
    back = [lax.ppermute(p, ("node", "head"), r) for p, r in zip(far_grads, routes)]
    mq = exchange(mq, downward)
    merged = call(functools.partial(merge_kernel, heads), "merge", [block] * heads, slots, near, *back)
    kv_grads = exchange(merged, order)
    unpack = functools.partial(unpack_kernel, heads)
    mq_places = [(downward.index(d), 0) for d in range(heads)]
    mixed, query_grad = call(functools.partial(unpack, mq_places), "unpack", [whole] * 2, *mq)
    key_grad, value_grad = call(functools.partial(unpack, places), "unpack", [whole] * 2, *kv_grads)
    return mixed, query_grad, key_grad, value_grad


def solution(mesh):
    rows = P(("grp", "node", "head"), None)
    return jax.shard_map(
        shards,
        mesh=mesh,
        in_specs=(rows, rows, rows, rows, P("grp", None)),
        out_specs=(rows, rows, rows, rows),
        check_vma=False,
    )
```

```python
import functools
import math

import jax
import jax.numpy as jnp
from jax import lax
from jax.experimental import pallas as pl
from jax.experimental.pallas import tpu as pltpu
from jax.sharding import PartitionSpec as P

HEAD_DIM = 64
NEVER = -1e30
SCORE_SCALE = HEAD_DIM**-0.5 / math.log(2)
LOW = jnp.bfloat16
VMEM = pl.BlockSpec(memory_space=pltpu.VMEM)
SMEM = pl.BlockSpec(memory_space=pltpu.SMEM)


def dot(left, right):
    return jnp.dot(left, right, preferred_element_type=jnp.float32)


def call(kernel, name, outs, *args, limit=8, scratch=(), cost=None, specs=None):
    return pl.pallas_call(
        kernel,
        out_shape=outs,
        in_specs=specs or [VMEM] * len(args),
        out_specs=[VMEM] * len(outs),
        scratch_shapes=scratch,
        name=name,
        cost_estimate=cost,
        compiler_params=pltpu.CompilerParams(vmem_limit_bytes=limit * 1024 * 1024),
    )(*args)


def partners(node):
    turn = 1 - 2 * (node % 2)
    return node + turn, node - turn


def pair_routes(owners, heads):
    routes = []
    for step in range(2):
        route = []
        for n in range(owners):
            other = partners(n)[step]
            for h in range(heads):
                target = other * heads + h if 0 <= other < owners else n * heads + (h ^ 1)
                route.append((n * heads + h, target))
        routes.append(route)
    return routes


def prep_kernel(heads, owners, local_count, per_patch, rows, nbr_ref, after_ref, bias_ref, slot_ref):
    me, node = lax.axis_index("head"), lax.axis_index("node")
    pair = partners(node)
    queries = heads * rows
    own = [[jnp.int32(p == k) for k in range(local_count)] for p in range(local_count)]
    out_of = [[jnp.int32(0), jnp.int32(0)] for _ in range(local_count)]
    for p in range(local_count):
        for j in range(nbr_ref.shape[1]):
            entry = nbr_ref[node * local_count + p, j]
            for k in range(local_count):
                own[p][k] += jnp.where(entry == node * local_count + k, 1, 0)
            for s in range(2):
                start = pair[s] * local_count
                inside = jnp.logical_and(entry >= start, entry < start + local_count)
                out_of[p][s] += jnp.where(inside, 1, 0)

    def choose(index, values):
        value = values[0]
        for i in range(1, len(values)):
            value = jnp.where(index == i, values[i], value)
        return value

    patch_of = [(me ^ d) // per_patch for d in range(heads)]
    counts = [
        [choose(patch_of[e], [choose(patch_of[d], own[p]) for p in range(local_count)]) for e in range(heads)]
        for d in range(heads)
    ]
    for s in range(2):
        counts.append([choose(patch_of[e], [out_of[p][s] for p in range(local_count)]) for e in range(heads)])
    lane_block = lax.broadcasted_iota(jnp.int32, (1, queries), 1) // rows
    for b, row_counts in enumerate(counts):
        row = jnp.zeros((1, queries), jnp.float32)
        for e in range(heads):
            row = jnp.where(lane_block == e, row_counts[e].astype(jnp.float32), row)
        row = jnp.where(row > 0.5, jnp.log(jnp.maximum(row, 1.0)) * (1 / math.log(2)), NEVER)
        bias_ref[b : b + 1, :] = row
    for s in range(2):
        inside = jnp.logical_and(pair[s] >= 0, pair[s] < owners)
        first = jnp.where(inside, pair[s], 0) * local_count
        chosen = jnp.int32(0)
        for p in range(local_count):
            for j in range(nbr_ref.shape[1]):
                entry = nbr_ref[first + p, j] - node * local_count
                mine = jnp.logical_and(entry >= 0, entry < local_count)
                chosen = jnp.where(jnp.logical_and(inside, mine), entry, chosen)
        for t in range(per_patch):
            slot = me ^ (chosen * per_patch + t)
            slot_ref[s * per_patch + t : s * per_patch + t + 1, :] = jnp.full((1, slot_ref.shape[1]), slot)


def pack_kernel(heads, one, two, *refs):
    me = lax.axis_index("head")
    width = refs[-1].shape[-1]
    for d, out in enumerate(refs[-heads:]):
        cols = pl.ds(pl.multiple_of((me ^ d) * width, width), width)
        out[0, 0], out[0, 1] = one[:, cols], two[:, cols]


def pick_kernel(heads, places, slot_ref, *refs):
    arrays, outs = refs[:-2], refs[-2:]
    rows = arrays[0].shape[2]
    per_patch = outs[0].shape[1] // rows
    blocks = [arrays[a][j].astype(jnp.float32) for a, j in places]
    for s, out in enumerate(outs):
        for t in range(per_patch):
            slot = slot_ref[s * per_patch + t : s * per_patch + t + 1, :]
            value = blocks[0]
            for d in range(1, heads):
                value = jnp.where((slot == d)[None], blocks[d], value)
            out[:, t * rows : (t + 1) * rows, :] = value.astype(LOW)


def spread(bias_ref, first, sizes):
    queries = bias_ref.shape[1]
    rows = [jnp.broadcast_to(bias_ref[first + i : first + i + 1, :], (n, queries)) for i, n in enumerate(sizes)]
    return jnp.concatenate(rows, 0)


def joined(arrays, places, which):
    return jnp.concatenate([arrays[a][j, which] for a, j in places], 0)


def near_kernel(heads, places, count, bias_ref, *refs):
    kv, qg, outs = refs[:count], refs[count : 2 * count], refs[2 * count :]
    exps_ref, gw_ref, stat_ref, *sides = outs
    rows, width = kv[0].shape[2:]
    queries = heads * rows
    groups = width // HEAD_DIM
    bias = spread(bias_ref, 0, [rows] * heads)
    keys, values = joined(kv, places, 0), joined(kv, places, 1)
    lane_head = lax.broadcasted_iota(jnp.int32, (1, width), 1) // HEAD_DIM
    for which, (down, across) in enumerate((sides[:2], sides[2:])):
        whole = joined(qg, places, which)
        turned = whole.T
        across[...] = jnp.zeros_like(across)
        for head in range(groups):
            feats = slice(head * HEAD_DIM, (head + 1) * HEAD_DIM)
            lanes = slice(head * queries, (head + 1) * queries)
            down[lanes, :] = jnp.where(lane_head == head, whole, jnp.zeros_like(whole))
            across[feats, lanes] = turned[feats]
    for head in range(groups):
        lanes = slice(head * queries, (head + 1) * queries)
        scores = dot(keys, sides[1][:, lanes]) * SCORE_SCALE + bias
        top = jnp.max(scores, 0, keepdims=True)
        exps = jnp.exp2(scores - top)
        grad_weights = dot(values, sides[3][:, lanes])
        exps_ref[:, lanes] = exps
        gw_ref[:, lanes] = grad_weights
        stat_ref[0:1, lanes] = top
        stat_ref[1:2, lanes] = jnp.sum(exps, 0, keepdims=True)
        stat_ref[2:3, lanes] = jnp.sum(exps * grad_weights, 0, keepdims=True)


def first_kernel(heads, bias_ref, query_across, grad_across, keys_ref, exps_ref, gw_ref, stat_ref):
    queries = bias_ref.shape[1]
    patch, width = keys_ref.shape[1:]
    bias = spread(bias_ref, heads, [patch])
    for head in range(width // HEAD_DIM):
        lanes = slice(head * queries, (head + 1) * queries)
        scores = dot(keys_ref[0], query_across[:, lanes]) * SCORE_SCALE + bias
        top = jnp.max(scores, 0, keepdims=True)
        exps = jnp.where(bias > NEVER, jnp.exp2(scores - top), 0.0)
        grad_weights = dot(keys_ref[1], grad_across[:, lanes])
        exps_ref[:, lanes] = exps
        gw_ref[:, lanes] = grad_weights
        stat_ref[0:1, lanes] = top
        stat_ref[1:2, lanes] = jnp.sum(exps, 0, keepdims=True)
        stat_ref[2:3, lanes] = jnp.sum(exps * grad_weights, 0, keepdims=True)


def far_kernel(heads, owners, bias_ref, stat_ref, exps_ref, gw_ref, first_ref, query_down, query_across, grad_down, *refs):
    grad_across, second_ref, w_ref, ds_ref, final_ref, far_a, far_b = refs
    patch, width = second_ref.shape[1:]
    queries = bias_ref.shape[1]
    node = lax.axis_index("node")
    other = partners(node)[1]
    both = jnp.logical_and(other >= 0, other < owners)

    def softmax(second):
        bias = spread(bias_ref, heads + 1, [patch]) if second else None
        for head in range(width // HEAD_DIM):
            lanes = slice(head * queries, (head + 1) * queries)
            near_top, first_top = stat_ref[0:1, lanes], first_ref[0:1, lanes]
            top = jnp.maximum(near_top, first_top)
            if second:
                scores = dot(second_ref[0], query_across[:, lanes]) * SCORE_SCALE + bias
                top = jnp.maximum(top, jnp.max(scores, 0, keepdims=True))
                exps = jnp.exp2(scores - top)
                grad_weights = dot(second_ref[1], grad_across[:, lanes])
            shrink, first_shrink = jnp.exp2(near_top - top), jnp.exp2(first_top - top)
            total = shrink * stat_ref[1:2, lanes] + first_shrink * first_ref[1:2, lanes]
            if second:
                total = total + jnp.sum(exps, 0, keepdims=True)
            part = 1.0 / total
            shrink, first_shrink = shrink * part, first_shrink * part
            row_dots = shrink * stat_ref[2:3, lanes] + first_shrink * first_ref[2:3, lanes]
            if second:
                weights = exps * part
                row_dots = row_dots + jnp.sum(weights * grad_weights, 0, keepdims=True)
                w_ref[patch:, lanes] = weights.astype(LOW)
                ds_ref[patch:, lanes] = (weights * (grad_weights - row_dots)).astype(LOW)
            weights = exps_ref[:, lanes] * first_shrink
            w_ref[:patch, lanes] = weights.astype(LOW)
            ds_ref[:patch, lanes] = (weights * (gw_ref[:, lanes] - row_dots)).astype(LOW)
            final_ref[0:1, lanes] = shrink
            final_ref[1:2, lanes] = row_dots

    @pl.when(both)
    def _():
        softmax(True)
        key_grad = dot(ds_ref[...], query_down[...]) * HEAD_DIM**-0.5
        value_grad = dot(w_ref[...], grad_down[...])
        for s, out in enumerate((far_a, far_b)):
            span = slice(s * patch, (s + 1) * patch)
            out[0], out[1] = key_grad[span].astype(LOW), value_grad[span].astype(LOW)

    @pl.when(jnp.logical_not(both))
    def _():
        softmax(False)
        far_a[0] = (dot(ds_ref[:patch, :], query_down[...]) * HEAD_DIM**-0.5).astype(LOW)
        far_a[1] = dot(w_ref[:patch, :], grad_down[...]).astype(LOW)
        far_b[...] = jnp.zeros_like(far_b)
        w_ref[patch:, :] = jnp.zeros((patch, w_ref.shape[1]), LOW)
        ds_ref[patch:, :] = jnp.zeros((patch, ds_ref.shape[1]), LOW)


def rest_kernel(heads, places, final_ref, exps_ref, gw_ref, far_w_ref, far_ds_ref, query_down, grad_down, *refs):
    kv, far, outs = refs[:heads], refs[heads : heads + 2], refs[heads + 2 : -3]
    near_out, w_ref, ds_ref = refs[-3:]
    rows, width = kv[0].shape[2:]
    queries = heads * rows
    keys_t, values_t = joined(kv, places, 0).T, joined(kv, places, 1).T
    far_keys_t = jnp.concatenate([r[0] for r in far], 0).T
    far_values_t = jnp.concatenate([r[1] for r in far], 0).T
    mixed_t, qgrad_t = [], []
    for head in range(width // HEAD_DIM):
        feats = slice(head * HEAD_DIM, (head + 1) * HEAD_DIM)
        lanes = slice(head * queries, (head + 1) * queries)
        weights = exps_ref[:, lanes] * final_ref[0:1, lanes]
        low = weights.astype(LOW)
        grad_scores = (weights * (gw_ref[:, lanes] - final_ref[1:2, lanes])).astype(LOW)
        w_ref[:, lanes] = low
        ds_ref[:, lanes] = grad_scores
        mixed_t.append(dot(values_t[feats], low) + dot(far_values_t[feats], far_w_ref[:, lanes]))
        qgrad_t.append((dot(keys_t[feats], grad_scores) + dot(far_keys_t[feats], far_ds_ref[:, lanes])) * HEAD_DIM**-0.5)
    mixed = jnp.concatenate(mixed_t, 0).T.astype(LOW)
    qgrad = jnp.concatenate(qgrad_t, 0).T.astype(LOW)
    key_grad = dot(ds_ref[...], query_down[...]) * HEAD_DIM**-0.5
    value_grad = dot(w_ref[...], grad_down[...])
    for d, out in enumerate(outs):
        span = slice(d * rows, (d + 1) * rows)
        out[0, 0], out[0, 1] = mixed[span], qgrad[span]
        near_out[d, 0], near_out[d, 1] = key_grad[span], value_grad[span]


def merge_kernel(heads, slot_ref, near, back_a, back_b, *outs):
    rows = near.shape[2]
    per_patch = back_a.shape[1] // rows
    me = lax.axis_index("head")
    for d in range(heads):
        total = near[d]
        part = lax.rem(me ^ d, per_patch)
        for s, back in enumerate((back_a, back_b)):
            slot = slot_ref[pl.ds(s * per_patch + part, 1), :]
            term = back[:, pl.ds(pl.multiple_of(part * rows, rows), rows), :].astype(jnp.float32)
            total = total + jnp.where((slot == d)[None], term, 0.0)
        outs[d][0] = total.astype(LOW)


def join_kernel(*refs):
    count = len(refs) // 3
    for i, out in enumerate(refs[2 * count :]):
        out[0, 0], out[0, 1] = refs[2 * i][...], refs[2 * i + 1][...]


def unpack_kernel(heads, places, *refs):
    arrays, outs = refs[:-2], refs[-2:]
    width = arrays[0].shape[-1]
    me = lax.axis_index("head")
    for d, (a, j) in enumerate(places):
        cols = pl.ds(pl.multiple_of((me ^ d) * width, width), width)
        outs[0][:, cols], outs[1][:, cols] = arrays[a][j, 0], arrays[a][j, 1]


def far_first(heads):
    return [0] + sorted(range(1, heads), key=lambda d: (-(d >> 1), d))


def exchange(blocks, order):
    heads = len(blocks)
    swaps = [[(i, i ^ d) for i in range(heads)] for d in range(heads)]
    return [lax.ppermute(blocks[d], "head", swaps[d]) if d else blocks[0] for d in order]


def cut(one, two, heads):
    me = lax.axis_index("head")
    width = one.shape[1] // heads
    starts = [(me ^ d) * width for d in range(heads)]
    parts = [[lax.dynamic_slice_in_dim(a, at, width, 1) for a in (one, two)] for at in starts]
    return call(join_kernel, "join", [jax.ShapeDtypeStruct((1, 2) + parts[0][0].shape, LOW)] * heads, *sum(parts, []))


def shards(queries, key_rows, value_rows, out_grads, neighbours):
    rows, features = queries.shape
    heads, owners = lax.axis_size("head"), lax.axis_size("node")
    width = features // heads
    local_count = neighbours.shape[0] // owners
    per_patch = heads // local_count
    patch = rows * per_patch
    block = jax.ShapeDtypeStruct((1, 2, rows, width), LOW)
    order, downward = far_first(heads), [0] + list(range(heads - 1, 0, -1))
    places = [(order.index(d), 0) for d in range(heads)]
    near_shape = jax.ShapeDtypeStruct((heads, 2, rows, width), jnp.float32)
    slab = jax.ShapeDtypeStruct((2, patch, width), LOW)
    whole = jax.ShapeDtypeStruct((rows, features), LOW)
    routes = pair_routes(owners, heads)

    kv = exchange(cut(key_rows, value_rows, heads), order)
    bias, slots = call(
        functools.partial(prep_kernel, heads, owners, local_count, per_patch, rows),
        "prep",
        [
            jax.ShapeDtypeStruct((heads + 2, heads * rows), jnp.float32),
            jax.ShapeDtypeStruct((2 * per_patch, width), jnp.int32),
        ],
        neighbours,
        kv[0],
        specs=[SMEM, VMEM],
    )
    pack = functools.partial(pack_kernel, heads)
    qg = exchange(call(pack, "pack", [block] * heads, queries, out_grads, slots), order)
    picked = call(functools.partial(pick_kernel, heads, places), "pick", [slab] * 2, slots, *kv)
    far = [lax.ppermute(p, ("node", "head"), r) for p, r in zip(picked, routes)]
    lanes = width // HEAD_DIM * heads * rows
    own, other = heads * rows, 2 * patch
    work = pl.CostEstimate(flops=1500000000, bytes_accessed=1, transcendentals=0)

    def table(height, kind=jnp.float32):
        return jax.ShapeDtypeStruct((height, lanes), kind)

    down = jax.ShapeDtypeStruct((lanes, width), LOW)
    across = jax.ShapeDtypeStruct((width, lanes), LOW)
    exps, grad_weights, stats, *sides = call(
        functools.partial(near_kernel, heads, places, len(kv)),
        "near",
        [table(own), table(own), table(3), down, across, down, across],
        bias,
        *kv,
        *qg,
        cost=work,
    )
    first = call(
        functools.partial(first_kernel, heads),
        "first",
        [table(patch), table(patch), table(3)],
        bias,
        sides[1],
        sides[3],
        far[0],
    )
    far_w, far_ds, final, *far_grads = call(
        functools.partial(far_kernel, heads, owners),
        "far",
        [table(other, LOW), table(other, LOW), table(2), slab, slab],
        bias,
        stats,
        *first,
        *sides,
        far[1],
        cost=work,
    )
    *mq, near = call(
        functools.partial(rest_kernel, heads, places),
        "rest",
        [block] * heads + [near_shape],
        final,
        exps,
        grad_weights,
        far_w,
        far_ds,
        sides[0],
        sides[2],
        *kv,
        *far,
        scratch=[pltpu.VMEM((own, lanes), LOW)] * 2,
        cost=work,
    )
    back = [lax.ppermute(p, ("node", "head"), r) for p, r in zip(far_grads, routes)]
    mq = exchange(mq, downward)
    merged = call(functools.partial(merge_kernel, heads), "merge", [block] * heads, slots, near, *back)
    kv_grads = exchange(merged, order)
    unpack = functools.partial(unpack_kernel, heads)
    mq_places = [(downward.index(d), 0) for d in range(heads)]
    mixed, query_grad = call(functools.partial(unpack, mq_places), "unpack", [whole] * 2, *mq)
    key_grad, value_grad = call(functools.partial(unpack, places), "unpack", [whole] * 2, *kv_grads)
    return mixed, query_grad, key_grad, value_grad


def solution(mesh):
    rows = P(("grp", "node", "head"), None)
    return jax.shard_map(
        shards,
        mesh=mesh,
        in_specs=(rows, rows, rows, rows, P("grp", None)),
        out_specs=(rows, rows, rows, rows),
        check_vma=False,
    )
```

```python
import functools
import math

import jax
import jax.numpy as jnp
from jax import lax
from jax.experimental import pallas as pl
from jax.experimental.pallas import tpu as pltpu
from jax.sharding import PartitionSpec as P

HEAD_DIM = 64
NEVER = -1e30
SCORE_SCALE = HEAD_DIM**-0.5 / math.log(2)
LOW = jnp.bfloat16
VMEM = pl.BlockSpec(memory_space=pltpu.VMEM)
SMEM = pl.BlockSpec(memory_space=pltpu.SMEM)


def dot(left, right):
    return jnp.dot(left, right, preferred_element_type=jnp.float32)


def call(kernel, name, outs, *args, limit=8, scratch=(), cost=None, specs=None):
    return pl.pallas_call(
        kernel,
        out_shape=outs,
        in_specs=specs or [VMEM] * len(args),
        out_specs=[VMEM] * len(outs),
        scratch_shapes=scratch,
        name=name,
        cost_estimate=cost,
        compiler_params=pltpu.CompilerParams(vmem_limit_bytes=limit * 1024 * 1024),
    )(*args)


def partners(node):
    turn = 1 - 2 * (node % 2)
    return node + turn, node - turn


def pair_routes(owners, heads):
    routes = []
    for step in range(2):
        route = []
        for n in range(owners):
            other = partners(n)[step]
            for h in range(heads):
                target = other * heads + h if 0 <= other < owners else n * heads + (h ^ 1)
                route.append((n * heads + h, target))
        routes.append(route)
    return routes


def prep_kernel(heads, owners, local_count, per_patch, rows, nbr_ref, after_ref, bias_ref, slot_ref):
    me, node = lax.axis_index("head"), lax.axis_index("node")
    pair = partners(node)
    queries = heads * rows
    own = [[jnp.int32(p == k) for k in range(local_count)] for p in range(local_count)]
    out_of = [[jnp.int32(0), jnp.int32(0)] for _ in range(local_count)]
    for p in range(local_count):
        for j in range(nbr_ref.shape[1]):
            entry = nbr_ref[node * local_count + p, j]
            for k in range(local_count):
                own[p][k] += jnp.where(entry == node * local_count + k, 1, 0)
            for s in range(2):
                start = pair[s] * local_count
                inside = jnp.logical_and(entry >= start, entry < start + local_count)
                out_of[p][s] += jnp.where(inside, 1, 0)

    def choose(index, values):
        value = values[0]
        for i in range(1, len(values)):
            value = jnp.where(index == i, values[i], value)
        return value

    patch_of = [(me ^ d) // per_patch for d in range(heads)]
    counts = [
        [choose(patch_of[e], [choose(patch_of[d], own[p]) for p in range(local_count)]) for e in range(heads)]
        for d in range(heads)
    ]
    for s in range(2):
        counts.append([choose(patch_of[e], [out_of[p][s] for p in range(local_count)]) for e in range(heads)])
    lane_block = lax.broadcasted_iota(jnp.int32, (1, queries), 1) // rows
    for b, row_counts in enumerate(counts):
        row = jnp.zeros((1, queries), jnp.float32)
        for e in range(heads):
            row = jnp.where(lane_block == e, row_counts[e].astype(jnp.float32), row)
        row = jnp.where(row > 0.5, jnp.log(jnp.maximum(row, 1.0)) * (1 / math.log(2)), NEVER)
        bias_ref[b : b + 1, :] = row
    for s in range(2):
        inside = jnp.logical_and(pair[s] >= 0, pair[s] < owners)
        first = jnp.where(inside, pair[s], 0) * local_count
        chosen = jnp.int32(0)
        for p in range(local_count):
            for j in range(nbr_ref.shape[1]):
                entry = nbr_ref[first + p, j] - node * local_count
                mine = jnp.logical_and(entry >= 0, entry < local_count)
                chosen = jnp.where(jnp.logical_and(inside, mine), entry, chosen)
        for t in range(per_patch):
            slot = me ^ (chosen * per_patch + t)
            slot_ref[s * per_patch + t : s * per_patch + t + 1, :] = jnp.full((1, slot_ref.shape[1]), slot)


def pack_kernel(heads, one, two, *refs):
    me = lax.axis_index("head")
    width = refs[-1].shape[-1]
    for d, out in enumerate(refs[-heads:]):
        cols = pl.ds(pl.multiple_of((me ^ d) * width, width), width)
        out[0, 0], out[0, 1] = one[:, cols], two[:, cols]


def pick_kernel(heads, places, slot_ref, *refs):
    arrays, outs = refs[:-2], refs[-2:]
    rows = arrays[0].shape[2]
    per_patch = outs[0].shape[1] // rows
    blocks = [arrays[a][j].astype(jnp.float32) for a, j in places]
    for s, out in enumerate(outs):
        for t in range(per_patch):
            slot = slot_ref[s * per_patch + t : s * per_patch + t + 1, :]
            value = blocks[0]
            for d in range(1, heads):
                value = jnp.where((slot == d)[None], blocks[d], value)
            out[:, t * rows : (t + 1) * rows, :] = value.astype(LOW)


def spread(bias_ref, first, sizes):
    queries = bias_ref.shape[1]
    rows = [jnp.broadcast_to(bias_ref[first + i : first + i + 1, :], (n, queries)) for i, n in enumerate(sizes)]
    return jnp.concatenate(rows, 0)


def joined(arrays, places, which):
    return jnp.concatenate([arrays[a][j, which] for a, j in places], 0)


def near_kernel(heads, places, count, bias_ref, *refs):
    kv, qg, outs = refs[:count], refs[count : 2 * count], refs[2 * count :]
    exps_ref, gw_ref, stat_ref, *sides = outs
    rows, width = kv[0].shape[2:]
    queries = heads * rows
    groups = width // HEAD_DIM
    bias = spread(bias_ref, 0, [rows] * heads)
    keys, values = joined(kv, places, 0), joined(kv, places, 1)
    lane_head = lax.broadcasted_iota(jnp.int32, (1, width), 1) // HEAD_DIM
    for which, (down, across) in enumerate((sides[:2], sides[2:])):
        whole = joined(qg, places, which)
        turned = whole.T
        across[...] = jnp.zeros_like(across)
        for head in range(groups):
            feats = slice(head * HEAD_DIM, (head + 1) * HEAD_DIM)
            lanes = slice(head * queries, (head + 1) * queries)
            down[lanes, :] = jnp.where(lane_head == head, whole, jnp.zeros_like(whole))
            across[feats, lanes] = turned[feats]
    for head in range(groups):
        lanes = slice(head * queries, (head + 1) * queries)
        scores = dot(keys, sides[1][:, lanes]) * SCORE_SCALE + bias
        top = jnp.max(scores, 0, keepdims=True)
        exps = jnp.exp2(scores - top)
        grad_weights = dot(values, sides[3][:, lanes])
        exps_ref[:, lanes] = exps
        gw_ref[:, lanes] = grad_weights
        stat_ref[0:1, lanes] = top
        stat_ref[1:2, lanes] = jnp.sum(exps, 0, keepdims=True)
        stat_ref[2:3, lanes] = jnp.sum(exps * grad_weights, 0, keepdims=True)


def first_kernel(heads, bias_ref, query_across, grad_across, keys_ref, exps_ref, gw_ref, stat_ref):
    queries = bias_ref.shape[1]
    patch, width = keys_ref.shape[1:]
    bias = spread(bias_ref, heads, [patch])
    for head in range(width // HEAD_DIM):
        lanes = slice(head * queries, (head + 1) * queries)
        scores = dot(keys_ref[0], query_across[:, lanes]) * SCORE_SCALE + bias
        top = jnp.max(scores, 0, keepdims=True)
        exps = jnp.where(bias > NEVER, jnp.exp2(scores - top), 0.0)
        grad_weights = dot(keys_ref[1], grad_across[:, lanes])
        exps_ref[:, lanes] = exps
        gw_ref[:, lanes] = grad_weights
        stat_ref[0:1, lanes] = top
        stat_ref[1:2, lanes] = jnp.sum(exps, 0, keepdims=True)
        stat_ref[2:3, lanes] = jnp.sum(exps * grad_weights, 0, keepdims=True)


def far_kernel(
    heads, owners, places, bias_ref, stat_ref, exps_ref, gw_ref, first_ref, query_down, query_across, grad_down, *refs
):
    grad_across, near_exps_ref, near_gw_ref = refs[:3]
    kv, slabs = refs[3 : heads + 3], refs[heads + 3 : heads + 5]
    w_ref, ds_ref, final_ref, far_a, far_b, *early, near_out, own_w_ref, own_ds_ref = refs[heads + 5 :]
    second_ref = slabs[1]
    patch, width = second_ref.shape[1:]
    queries = bias_ref.shape[1]
    node = lax.axis_index("node")
    other = partners(node)[1]
    both = jnp.logical_and(other >= 0, other < owners)

    def softmax(second):
        bias = spread(bias_ref, heads + 1, [patch]) if second else None
        for head in range(width // HEAD_DIM):
            lanes = slice(head * queries, (head + 1) * queries)
            near_top, first_top = stat_ref[0:1, lanes], first_ref[0:1, lanes]
            top = jnp.maximum(near_top, first_top)
            if second:
                scores = dot(second_ref[0], query_across[:, lanes]) * SCORE_SCALE + bias
                top = jnp.maximum(top, jnp.max(scores, 0, keepdims=True))
                exps = jnp.exp2(scores - top)
                grad_weights = dot(second_ref[1], grad_across[:, lanes])
            shrink, first_shrink = jnp.exp2(near_top - top), jnp.exp2(first_top - top)
            total = shrink * stat_ref[1:2, lanes] + first_shrink * first_ref[1:2, lanes]
            if second:
                total = total + jnp.sum(exps, 0, keepdims=True)
            part = 1.0 / total
            shrink, first_shrink = shrink * part, first_shrink * part
            row_dots = shrink * stat_ref[2:3, lanes] + first_shrink * first_ref[2:3, lanes]
            if second:
                weights = exps * part
                row_dots = row_dots + jnp.sum(weights * grad_weights, 0, keepdims=True)
                w_ref[patch:, lanes] = weights.astype(LOW)
                ds_ref[patch:, lanes] = (weights * (grad_weights - row_dots)).astype(LOW)
            weights = exps_ref[:, lanes] * first_shrink
            w_ref[:patch, lanes] = weights.astype(LOW)
            ds_ref[:patch, lanes] = (weights * (gw_ref[:, lanes] - row_dots)).astype(LOW)
            final_ref[0:1, lanes] = shrink
            final_ref[1:2, lanes] = row_dots

    @pl.when(both)
    def _():
        softmax(True)
        key_grad = dot(ds_ref[...], query_down[...]) * HEAD_DIM**-0.5
        value_grad = dot(w_ref[...], grad_down[...])
        for s, out in enumerate((far_a, far_b)):
            span = slice(s * patch, (s + 1) * patch)
            out[0], out[1] = key_grad[span].astype(LOW), value_grad[span].astype(LOW)

    @pl.when(jnp.logical_not(both))
    def _():
        softmax(False)
        far_a[0] = (dot(ds_ref[:patch, :], query_down[...]) * HEAD_DIM**-0.5).astype(LOW)
        far_a[1] = dot(w_ref[:patch, :], grad_down[...]).astype(LOW)
        far_b[...] = jnp.zeros_like(far_b)
        w_ref[patch:, :] = jnp.zeros((patch, w_ref.shape[1]), LOW)
        ds_ref[patch:, :] = jnp.zeros((patch, ds_ref.shape[1]), LOW)

    @pl.when(node == 0)
    def _():
        weights_of = final_ref, near_exps_ref, near_gw_ref, w_ref, ds_ref
        rest(places, weights_of, (query_down, grad_down), kv, slabs, early, near_out, own_w_ref, own_ds_ref)


def rest(places, weights_of, downs, kv, far, outs, near_out, w_ref, ds_ref):
    heads = len(places)
    final_ref, exps_ref, gw_ref, far_w_ref, far_ds_ref = weights_of
    query_down, grad_down = downs
    rows, width = kv[0].shape[2:]
    queries = heads * rows
    keys_t, values_t = joined(kv, places, 0).T, joined(kv, places, 1).T
    far_keys_t = jnp.concatenate([r[0] for r in far], 0).T
    far_values_t = jnp.concatenate([r[1] for r in far], 0).T
    mixed_t, qgrad_t = [], []
    for head in range(width // HEAD_DIM):
        feats = slice(head * HEAD_DIM, (head + 1) * HEAD_DIM)
        lanes = slice(head * queries, (head + 1) * queries)
        weights = exps_ref[:, lanes] * final_ref[0:1, lanes]
        low = weights.astype(LOW)
        grad_scores = (weights * (gw_ref[:, lanes] - final_ref[1:2, lanes])).astype(LOW)
        w_ref[:, lanes] = low
        ds_ref[:, lanes] = grad_scores
        mixed_t.append(dot(values_t[feats], low) + dot(far_values_t[feats], far_w_ref[:, lanes]))
        qgrad_t.append((dot(keys_t[feats], grad_scores) + dot(far_keys_t[feats], far_ds_ref[:, lanes])) * HEAD_DIM**-0.5)
    mixed = jnp.concatenate(mixed_t, 0).T.astype(LOW)
    qgrad = jnp.concatenate(qgrad_t, 0).T.astype(LOW)
    key_grad = dot(ds_ref[...], query_down[...]) * HEAD_DIM**-0.5
    value_grad = dot(w_ref[...], grad_down[...])
    for d, out in enumerate(outs):
        span = slice(d * rows, (d + 1) * rows)
        out[0, 0], out[0, 1] = mixed[span], qgrad[span]
        near_out[d, 0], near_out[d, 1] = key_grad[span], value_grad[span]


def rest_kernel(heads, places, final_ref, exps_ref, gw_ref, far_w_ref, far_ds_ref, query_down, grad_down, *refs):
    kv, far, early = refs[:heads], refs[heads : heads + 2], refs[heads + 2 : 2 * heads + 3]
    *outs, near_out, w_ref, ds_ref = refs[2 * heads + 3 :]
    first = lax.axis_index("node") == 0

    @pl.when(first)
    def _():
        for ref, out in zip(early, outs + [near_out]):
            out[...] = ref[...]

    @pl.when(jnp.logical_not(first))
    def _():
        weights_of = final_ref, exps_ref, gw_ref, far_w_ref, far_ds_ref
        rest(places, weights_of, (query_down, grad_down), kv, far, outs, near_out, w_ref, ds_ref)


def merge_kernel(heads, slot_ref, near, back_a, back_b, *outs):
    rows = near.shape[2]
    per_patch = back_a.shape[1] // rows
    me = lax.axis_index("head")
    for d in range(heads):
        total = near[d]
        part = lax.rem(me ^ d, per_patch)
        for s, back in enumerate((back_a, back_b)):
            slot = slot_ref[pl.ds(s * per_patch + part, 1), :]
            term = back[:, pl.ds(pl.multiple_of(part * rows, rows), rows), :].astype(jnp.float32)
            total = total + jnp.where((slot == d)[None], term, 0.0)
        outs[d][0] = total.astype(LOW)


def join_kernel(*refs):
    count = len(refs) // 3
    for i, out in enumerate(refs[2 * count :]):
        out[0, 0], out[0, 1] = refs[2 * i][...], refs[2 * i + 1][...]


def unpack_kernel(heads, places, *refs):
    arrays, outs = refs[:-2], refs[-2:]
    width = arrays[0].shape[-1]
    me = lax.axis_index("head")
    for d, (a, j) in enumerate(places):
        cols = pl.ds(pl.multiple_of((me ^ d) * width, width), width)
        outs[0][:, cols], outs[1][:, cols] = arrays[a][j, 0], arrays[a][j, 1]


def far_first(heads):
    return [0] + sorted(range(1, heads), key=lambda d: (-(d >> 1), d))


def exchange(blocks, order):
    heads = len(blocks)
    swaps = [[(i, i ^ d) for i in range(heads)] for d in range(heads)]
    return [lax.ppermute(blocks[d], "head", swaps[d]) if d else blocks[0] for d in order]


def cut(one, two, heads):
    me = lax.axis_index("head")
    width = one.shape[1] // heads
    starts = [(me ^ d) * width for d in range(heads)]
    parts = [[lax.dynamic_slice_in_dim(a, at, width, 1) for a in (one, two)] for at in starts]
    return call(join_kernel, "join", [jax.ShapeDtypeStruct((1, 2) + parts[0][0].shape, LOW)] * heads, *sum(parts, []))


def shards(queries, key_rows, value_rows, out_grads, neighbours):
    rows, features = queries.shape
    heads, owners = lax.axis_size("head"), lax.axis_size("node")
    width = features // heads
    local_count = neighbours.shape[0] // owners
    per_patch = heads // local_count
    patch = rows * per_patch
    block = jax.ShapeDtypeStruct((1, 2, rows, width), LOW)
    order, downward = far_first(heads), [0] + list(range(heads - 1, 0, -1))
    places = [(order.index(d), 0) for d in range(heads)]
    near_shape = jax.ShapeDtypeStruct((heads, 2, rows, width), jnp.float32)
    slab = jax.ShapeDtypeStruct((2, patch, width), LOW)
    whole = jax.ShapeDtypeStruct((rows, features), LOW)
    routes = pair_routes(owners, heads)

    kv = exchange(cut(key_rows, value_rows, heads), order)
    bias, slots = call(
        functools.partial(prep_kernel, heads, owners, local_count, per_patch, rows),
        "prep",
        [
            jax.ShapeDtypeStruct((heads + 2, heads * rows), jnp.float32),
            jax.ShapeDtypeStruct((2 * per_patch, width), jnp.int32),
        ],
        neighbours,
        kv[0],
        specs=[SMEM, VMEM],
    )
    pack = functools.partial(pack_kernel, heads)
    qg = exchange(call(pack, "pack", [block] * heads, queries, out_grads, slots), order)
    picked = call(functools.partial(pick_kernel, heads, places), "pick", [slab] * 2, slots, *kv)
    far = [lax.ppermute(p, ("node", "head"), r) for p, r in zip(picked, routes)]
    lanes = width // HEAD_DIM * heads * rows
    own, other = heads * rows, 2 * patch
    work = pl.CostEstimate(flops=1500000000, bytes_accessed=1, transcendentals=0)

    def table(height, kind=jnp.float32):
        return jax.ShapeDtypeStruct((height, lanes), kind)

    down = jax.ShapeDtypeStruct((lanes, width), LOW)
    across = jax.ShapeDtypeStruct((width, lanes), LOW)
    exps, grad_weights, stats, *sides = call(
        functools.partial(near_kernel, heads, places, len(kv)),
        "near",
        [table(own), table(own), table(3), down, across, down, across],
        bias,
        *kv,
        *qg,
        cost=work,
    )
    first = call(
        functools.partial(first_kernel, heads),
        "first",
        [table(patch), table(patch), table(3)],
        bias,
        sides[1],
        sides[3],
        far[0],
    )
    far_w, far_ds, final, far_a, far_b, *early = call(
        functools.partial(far_kernel, heads, owners, places),
        "far",
        [table(other, LOW), table(other, LOW), table(2), slab, slab] + [block] * heads + [near_shape],
        bias,
        stats,
        *first,
        *sides,
        exps,
        grad_weights,
        *kv,
        *far,
        scratch=[pltpu.VMEM((own, lanes), LOW)] * 2,
        limit=12,
        cost=work,
    )
    *mq, near = call(
        functools.partial(rest_kernel, heads, places),
        "rest",
        [block] * heads + [near_shape],
        final,
        exps,
        grad_weights,
        far_w,
        far_ds,
        sides[0],
        sides[2],
        *kv,
        *far,
        *early,
        scratch=[pltpu.VMEM((own, lanes), LOW)] * 2,
        cost=work,
    )
    back = [lax.ppermute(p, ("node", "head"), r) for p, r in zip((far_a, far_b), routes)]
    mq = exchange(mq, downward)
    merged = call(functools.partial(merge_kernel, heads), "merge", [block] * heads, slots, near, *back)
    kv_grads = exchange(merged, order)
    unpack = functools.partial(unpack_kernel, heads)
    mq_places = [(downward.index(d), 0) for d in range(heads)]
    mixed, query_grad = call(functools.partial(unpack, mq_places), "unpack", [whole] * 2, *mq)
    key_grad, value_grad = call(functools.partial(unpack, places), "unpack", [whole] * 2, *kv_grads)
    return mixed, query_grad, key_grad, value_grad


def solution(mesh):
    rows = P(("grp", "node", "head"), None)
    return jax.shard_map(
        shards,
        mesh=mesh,
        in_specs=(rows, rows, rows, rows, P("grp", None)),
        out_specs=(rows, rows, rows, rows),
        check_vma=False,
    )
```

```python
import functools
import math

import jax
import jax.numpy as jnp
from jax import lax
from jax.experimental import pallas as pl
from jax.experimental.pallas import tpu as pltpu
from jax.sharding import PartitionSpec as P

HEAD_DIM = 64
NEVER = -1e30
SCORE_SCALE = HEAD_DIM**-0.5 / math.log(2)
LOW = jnp.bfloat16
VMEM = pl.BlockSpec(memory_space=pltpu.VMEM)
SMEM = pl.BlockSpec(memory_space=pltpu.SMEM)


def dot(left, right):
    return jnp.dot(left, right, preferred_element_type=jnp.float32)


def call(kernel, name, outs, *args, limit=8, scratch=(), cost=None, specs=None):
    return pl.pallas_call(
        kernel,
        out_shape=outs,
        in_specs=specs or [VMEM] * len(args),
        out_specs=[VMEM] * len(outs),
        scratch_shapes=scratch,
        name=name,
        cost_estimate=cost,
        compiler_params=pltpu.CompilerParams(vmem_limit_bytes=limit * 1024 * 1024),
    )(*args)


def partners(node):
    turn = 1 - 2 * (node % 2)
    return node + turn, node - turn


def pair_routes(owners, heads):
    routes = []
    for step in range(2):
        route = []
        for n in range(owners):
            other = partners(n)[step]
            for h in range(heads):
                target = other * heads + h if 0 <= other < owners else n * heads + (h ^ 1)
                route.append((n * heads + h, target))
        routes.append(route)
    return routes


def prep_kernel(heads, owners, local_count, per_patch, rows, nbr_ref, after_ref, bias_ref, slot_ref):
    me, node = lax.axis_index("head"), lax.axis_index("node")
    pair = partners(node)
    queries = heads * rows
    own = [[jnp.int32(p == k) for k in range(local_count)] for p in range(local_count)]
    out_of = [[jnp.int32(0), jnp.int32(0)] for _ in range(local_count)]
    for p in range(local_count):
        for j in range(nbr_ref.shape[1]):
            entry = nbr_ref[node * local_count + p, j]
            for k in range(local_count):
                own[p][k] += jnp.where(entry == node * local_count + k, 1, 0)
            for s in range(2):
                start = pair[s] * local_count
                inside = jnp.logical_and(entry >= start, entry < start + local_count)
                out_of[p][s] += jnp.where(inside, 1, 0)

    def choose(index, values):
        value = values[0]
        for i in range(1, len(values)):
            value = jnp.where(index == i, values[i], value)
        return value

    patch_of = [(me ^ d) // per_patch for d in range(heads)]
    counts = [
        [choose(patch_of[e], [choose(patch_of[d], own[p]) for p in range(local_count)]) for e in range(heads)]
        for d in range(heads)
    ]
    for s in range(2):
        counts.append([choose(patch_of[e], [out_of[p][s] for p in range(local_count)]) for e in range(heads)])
    lane_block = lax.broadcasted_iota(jnp.int32, (1, queries), 1) // rows
    for b, row_counts in enumerate(counts):
        row = jnp.zeros((1, queries), jnp.float32)
        for e in range(heads):
            row = jnp.where(lane_block == e, row_counts[e].astype(jnp.float32), row)
        row = jnp.where(row > 0.5, jnp.log(jnp.maximum(row, 1.0)) * (1 / math.log(2)), NEVER)
        bias_ref[b : b + 1, :] = row
    for s in range(2):
        inside = jnp.logical_and(pair[s] >= 0, pair[s] < owners)
        first = jnp.where(inside, pair[s], 0) * local_count
        chosen = jnp.int32(0)
        for p in range(local_count):
            for j in range(nbr_ref.shape[1]):
                entry = nbr_ref[first + p, j] - node * local_count
                mine = jnp.logical_and(entry >= 0, entry < local_count)
                chosen = jnp.where(jnp.logical_and(inside, mine), entry, chosen)
        for t in range(per_patch):
            slot = me ^ (chosen * per_patch + t)
            slot_ref[s * per_patch + t : s * per_patch + t + 1, :] = jnp.full((1, slot_ref.shape[1]), slot)


def pack_kernel(heads, one, two, *refs):
    me = lax.axis_index("head")
    width = refs[-1].shape[-1]
    for d, out in enumerate(refs[-heads:]):
        cols = pl.ds(pl.multiple_of((me ^ d) * width, width), width)
        out[0, 0], out[0, 1] = one[:, cols], two[:, cols]


def pick_kernel(heads, places, slot_ref, *refs):
    arrays, outs = refs[:-2], refs[-2:]
    rows = arrays[0].shape[2]
    per_patch = outs[0].shape[1] // rows
    blocks = [arrays[a][j].astype(jnp.float32) for a, j in places]
    for s, out in enumerate(outs):
        for t in range(per_patch):
            slot = slot_ref[s * per_patch + t : s * per_patch + t + 1, :]
            value = blocks[0]
            for d in range(1, heads):
                value = jnp.where((slot == d)[None], blocks[d], value)
            out[:, t * rows : (t + 1) * rows, :] = value.astype(LOW)


def spread(bias_ref, first, sizes):
    queries = bias_ref.shape[1]
    rows = [jnp.broadcast_to(bias_ref[first + i : first + i + 1, :], (n, queries)) for i, n in enumerate(sizes)]
    return jnp.concatenate(rows, 0)


def joined(arrays, places, which):
    return jnp.concatenate([arrays[a][j, which] for a, j in places], 0)


def near_kernel(heads, places, count, bias_ref, *refs):
    kv, qg, outs = refs[:count], refs[count : 2 * count], refs[2 * count :]
    exps_ref, gw_ref, stat_ref, *sides = outs
    rows, width = kv[0].shape[2:]
    queries = heads * rows
    groups = width // HEAD_DIM
    bias = spread(bias_ref, 0, [rows] * heads)
    keys, values = joined(kv, places, 0), joined(kv, places, 1)
    lane_head = lax.broadcasted_iota(jnp.int32, (1, width), 1) // HEAD_DIM
    for which, (down, across) in enumerate((sides[:2], sides[2:])):
        whole = joined(qg, places, which)
        turned = whole.T
        across[...] = jnp.zeros_like(across)
        for head in range(groups):
            feats = slice(head * HEAD_DIM, (head + 1) * HEAD_DIM)
            lanes = slice(head * queries, (head + 1) * queries)
            down[lanes, :] = jnp.where(lane_head == head, whole, jnp.zeros_like(whole))
            across[feats, lanes] = turned[feats]
    for head in range(groups):
        lanes = slice(head * queries, (head + 1) * queries)
        scores = dot(keys, sides[1][:, lanes]) * SCORE_SCALE + bias
        top = jnp.max(scores, 0, keepdims=True)
        exps = jnp.exp2(scores - top)
        grad_weights = dot(values, sides[3][:, lanes])
        exps_ref[:, lanes] = exps
        gw_ref[:, lanes] = grad_weights
        stat_ref[0:1, lanes] = top
        stat_ref[1:2, lanes] = jnp.sum(exps, 0, keepdims=True)
        stat_ref[2:3, lanes] = jnp.sum(exps * grad_weights, 0, keepdims=True)


def first_kernel(heads, bias_ref, query_across, grad_across, keys_ref, exps_ref, gw_ref, stat_ref):
    queries = bias_ref.shape[1]
    patch, width = keys_ref.shape[1:]
    bias = spread(bias_ref, heads, [patch])
    for head in range(width // HEAD_DIM):
        lanes = slice(head * queries, (head + 1) * queries)
        scores = dot(keys_ref[0], query_across[:, lanes]) * SCORE_SCALE + bias
        top = jnp.max(scores, 0, keepdims=True)
        exps = jnp.where(bias > NEVER, jnp.exp2(scores - top), 0.0)
        grad_weights = dot(keys_ref[1], grad_across[:, lanes])
        exps_ref[:, lanes] = exps
        gw_ref[:, lanes] = grad_weights
        stat_ref[0:1, lanes] = top
        stat_ref[1:2, lanes] = jnp.sum(exps, 0, keepdims=True)
        stat_ref[2:3, lanes] = jnp.sum(exps * grad_weights, 0, keepdims=True)


def far_kernel(
    heads, owners, places, bias_ref, stat_ref, exps_ref, gw_ref, first_ref, query_down, query_across, grad_down, *refs
):
    grad_across, near_exps_ref, near_gw_ref = refs[:3]
    kv, slabs = refs[3 : heads + 3], refs[heads + 3 : heads + 5]
    w_ref, ds_ref, final_ref, far_a, far_b, *early, near_out, own_w_ref, own_ds_ref = refs[heads + 5 :]
    second_ref = slabs[1]
    patch, width = second_ref.shape[1:]
    queries = bias_ref.shape[1]
    node = lax.axis_index("node")
    other = partners(node)[1]
    both = jnp.logical_and(other >= 0, other < owners)

    def softmax(second):
        bias = spread(bias_ref, heads + 1, [patch]) if second else None
        for head in range(width // HEAD_DIM):
            lanes = slice(head * queries, (head + 1) * queries)
            near_top, first_top = stat_ref[0:1, lanes], first_ref[0:1, lanes]
            top = jnp.maximum(near_top, first_top)
            if second:
                scores = dot(second_ref[0], query_across[:, lanes]) * SCORE_SCALE + bias
                top = jnp.maximum(top, jnp.max(scores, 0, keepdims=True))
                exps = jnp.exp2(scores - top)
                grad_weights = dot(second_ref[1], grad_across[:, lanes])
            shrink, first_shrink = jnp.exp2(near_top - top), jnp.exp2(first_top - top)
            total = shrink * stat_ref[1:2, lanes] + first_shrink * first_ref[1:2, lanes]
            if second:
                total = total + jnp.sum(exps, 0, keepdims=True)
            part = 1.0 / total
            shrink, first_shrink = shrink * part, first_shrink * part
            row_dots = shrink * stat_ref[2:3, lanes] + first_shrink * first_ref[2:3, lanes]
            if second:
                weights = exps * part
                row_dots = row_dots + jnp.sum(weights * grad_weights, 0, keepdims=True)
                w_ref[patch:, lanes] = weights.astype(LOW)
                ds_ref[patch:, lanes] = (weights * (grad_weights - row_dots)).astype(LOW)
            weights = exps_ref[:, lanes] * first_shrink
            w_ref[:patch, lanes] = weights.astype(LOW)
            ds_ref[:patch, lanes] = (weights * (gw_ref[:, lanes] - row_dots)).astype(LOW)
            final_ref[0:1, lanes] = shrink
            final_ref[1:2, lanes] = row_dots

    @pl.when(both)
    def _():
        softmax(True)
        key_grad = dot(ds_ref[...], query_down[...]) * HEAD_DIM**-0.5
        value_grad = dot(w_ref[...], grad_down[...])
        for s, out in enumerate((far_a, far_b)):
            span = slice(s * patch, (s + 1) * patch)
            out[0], out[1] = key_grad[span].astype(LOW), value_grad[span].astype(LOW)

    @pl.when(jnp.logical_not(both))
    def _():
        softmax(False)
        far_a[0] = (dot(ds_ref[:patch, :], query_down[...]) * HEAD_DIM**-0.5).astype(LOW)
        far_a[1] = dot(w_ref[:patch, :], grad_down[...]).astype(LOW)
        far_b[...] = jnp.zeros_like(far_b)
        w_ref[patch:, :] = jnp.zeros((patch, w_ref.shape[1]), LOW)
        ds_ref[patch:, :] = jnp.zeros((patch, ds_ref.shape[1]), LOW)

    @pl.when(node == 0)
    def _():
        weights_of = final_ref, near_exps_ref, near_gw_ref, w_ref, ds_ref
        rest(places, weights_of, (query_down, grad_down), kv, slabs, early, near_out, own_w_ref, own_ds_ref)


def rest(places, weights_of, downs, kv, far, outs, near_out, w_ref, ds_ref):
    heads = len(places)
    final_ref, exps_ref, gw_ref, far_w_ref, far_ds_ref = weights_of
    query_down, grad_down = downs
    rows, width = kv[0].shape[2:]
    queries = heads * rows
    keys_t, values_t = joined(kv, places, 0).T, joined(kv, places, 1).T
    far_keys_t = jnp.concatenate([r[0] for r in far], 0).T
    far_values_t = jnp.concatenate([r[1] for r in far], 0).T
    mixed_t, qgrad_t = [], []
    for head in range(width // HEAD_DIM):
        feats = slice(head * HEAD_DIM, (head + 1) * HEAD_DIM)
        lanes = slice(head * queries, (head + 1) * queries)
        weights = exps_ref[:, lanes] * final_ref[0:1, lanes]
        low = weights.astype(LOW)
        grad_scores = (weights * (gw_ref[:, lanes] - final_ref[1:2, lanes])).astype(LOW)
        w_ref[:, lanes] = low
        ds_ref[:, lanes] = grad_scores
        mixed_t.append(dot(values_t[feats], low) + dot(far_values_t[feats], far_w_ref[:, lanes]))
        qgrad_t.append((dot(keys_t[feats], grad_scores) + dot(far_keys_t[feats], far_ds_ref[:, lanes])) * HEAD_DIM**-0.5)
    mixed = jnp.concatenate(mixed_t, 0).T.astype(LOW)
    qgrad = jnp.concatenate(qgrad_t, 0).T.astype(LOW)
    key_grad = dot(ds_ref[...], query_down[...]) * HEAD_DIM**-0.5
    value_grad = dot(w_ref[...], grad_down[...])
    for d, out in enumerate(outs):
        span = slice(d * rows, (d + 1) * rows)
        out[0, 0], out[0, 1] = mixed[span], qgrad[span]
        near_out[d, 0], near_out[d, 1] = key_grad[span].astype(LOW), value_grad[span].astype(LOW)


def rest_kernel(heads, places, final_ref, exps_ref, gw_ref, far_w_ref, far_ds_ref, query_down, grad_down, *refs):
    kv, far, early = refs[:heads], refs[heads : heads + 2], refs[heads + 2 : 2 * heads + 3]
    *outs, near_out, w_ref, ds_ref = refs[2 * heads + 3 :]
    first = lax.axis_index("node") == 0

    @pl.when(first)
    def _():
        for ref, out in zip(early, outs + [near_out]):
            out[...] = ref[...]

    @pl.when(jnp.logical_not(first))
    def _():
        weights_of = final_ref, exps_ref, gw_ref, far_w_ref, far_ds_ref
        rest(places, weights_of, (query_down, grad_down), kv, far, outs, near_out, w_ref, ds_ref)


def merge_kernel(heads, slot_ref, near, back_a, back_b, *outs):
    rows = near.shape[2]
    per_patch = back_a.shape[1] // rows
    me = lax.axis_index("head")
    for d in range(heads):
        total = near[d].astype(jnp.float32)
        part = lax.rem(me ^ d, per_patch)
        for s, back in enumerate((back_a, back_b)):
            slot = slot_ref[pl.ds(s * per_patch + part, 1), :]
            term = back[:, pl.ds(pl.multiple_of(part * rows, rows), rows), :].astype(jnp.float32)
            total = total + jnp.where((slot == d)[None], term, 0.0)
        outs[d][0] = total.astype(LOW)


def join_kernel(*refs):
    count = len(refs) // 3
    for i, out in enumerate(refs[2 * count :]):
        out[0, 0], out[0, 1] = refs[2 * i][...], refs[2 * i + 1][...]


def unpack_kernel(heads, places, *refs):
    arrays, outs = refs[:-2], refs[-2:]
    width = arrays[0].shape[-1]
    me = lax.axis_index("head")
    for d, (a, j) in enumerate(places):
        cols = pl.ds(pl.multiple_of((me ^ d) * width, width), width)
        outs[0][:, cols], outs[1][:, cols] = arrays[a][j, 0], arrays[a][j, 1]


def far_first(heads):
    return [0] + sorted(range(1, heads), key=lambda d: (-(d >> 1), d))


def exchange(blocks, order):
    heads = len(blocks)
    swaps = [[(i, i ^ d) for i in range(heads)] for d in range(heads)]
    return [lax.ppermute(blocks[d], "head", swaps[d]) if d else blocks[0] for d in order]


def cut(one, two, heads):
    me = lax.axis_index("head")
    width = one.shape[1] // heads
    starts = [(me ^ d) * width for d in range(heads)]
    parts = [[lax.dynamic_slice_in_dim(a, at, width, 1) for a in (one, two)] for at in starts]
    return call(join_kernel, "join", [jax.ShapeDtypeStruct((1, 2) + parts[0][0].shape, LOW)] * heads, *sum(parts, []))


def shards(queries, key_rows, value_rows, out_grads, neighbours):
    rows, features = queries.shape
    heads, owners = lax.axis_size("head"), lax.axis_size("node")
    width = features // heads
    local_count = neighbours.shape[0] // owners
    per_patch = heads // local_count
    patch = rows * per_patch
    block = jax.ShapeDtypeStruct((1, 2, rows, width), LOW)
    order, downward = far_first(heads), [0] + list(range(heads - 1, 0, -1))
    places = [(order.index(d), 0) for d in range(heads)]
    near_shape = jax.ShapeDtypeStruct((heads, 2, rows, width), LOW)
    slab = jax.ShapeDtypeStruct((2, patch, width), LOW)
    whole = jax.ShapeDtypeStruct((rows, features), LOW)
    routes = pair_routes(owners, heads)

    kv = exchange(cut(key_rows, value_rows, heads), order)
    bias, slots = call(
        functools.partial(prep_kernel, heads, owners, local_count, per_patch, rows),
        "prep",
        [
            jax.ShapeDtypeStruct((heads + 2, heads * rows), jnp.float32),
            jax.ShapeDtypeStruct((2 * per_patch, width), jnp.int32),
        ],
        neighbours,
        kv[0],
        specs=[SMEM, VMEM],
    )
    pack = functools.partial(pack_kernel, heads)
    qg = exchange(call(pack, "pack", [block] * heads, queries, out_grads, slots), order)
    picked = call(functools.partial(pick_kernel, heads, places), "pick", [slab] * 2, slots, *kv)
    far = [lax.ppermute(p, ("node", "head"), r) for p, r in zip(picked, routes)]
    lanes = width // HEAD_DIM * heads * rows
    own, other = heads * rows, 2 * patch
    work = pl.CostEstimate(flops=1500000000, bytes_accessed=1, transcendentals=0)

    def table(height, kind=jnp.float32):
        return jax.ShapeDtypeStruct((height, lanes), kind)

    down = jax.ShapeDtypeStruct((lanes, width), LOW)
    across = jax.ShapeDtypeStruct((width, lanes), LOW)
    exps, grad_weights, stats, *sides = call(
        functools.partial(near_kernel, heads, places, len(kv)),
        "near",
        [table(own), table(own), table(3), down, across, down, across],
        bias,
        *kv,
        *qg,
        cost=work,
    )
    first = call(
        functools.partial(first_kernel, heads),
        "first",
        [table(patch), table(patch), table(3)],
        bias,
        sides[1],
        sides[3],
        far[0],
    )
    far_w, far_ds, final, far_a, far_b, *early = call(
        functools.partial(far_kernel, heads, owners, places),
        "far",
        [table(other, LOW), table(other, LOW), table(2), slab, slab] + [block] * heads + [near_shape],
        bias,
        stats,
        *first,
        *sides,
        exps,
        grad_weights,
        *kv,
        *far,
        scratch=[pltpu.VMEM((own, lanes), LOW)] * 2,
        limit=12,
        cost=work,
    )
    *mq, near = call(
        functools.partial(rest_kernel, heads, places),
        "rest",
        [block] * heads + [near_shape],
        final,
        exps,
        grad_weights,
        far_w,
        far_ds,
        sides[0],
        sides[2],
        *kv,
        *far,
        *early,
        scratch=[pltpu.VMEM((own, lanes), LOW)] * 2,
        cost=work,
    )
    back = [lax.ppermute(p, ("node", "head"), r) for p, r in zip((far_a, far_b), routes)]
    mq = exchange(mq, downward)
    merged = call(functools.partial(merge_kernel, heads), "merge", [block] * heads, slots, near, *back)
    kv_grads = exchange(merged, order)
    unpack = functools.partial(unpack_kernel, heads)
    mq_places = [(downward.index(d), 0) for d in range(heads)]
    mixed, query_grad = call(functools.partial(unpack, mq_places), "unpack", [whole] * 2, *mq)
    key_grad, value_grad = call(functools.partial(unpack, places), "unpack", [whole] * 2, *kv_grads)
    return mixed, query_grad, key_grad, value_grad


def solution(mesh):
    rows = P(("grp", "node", "head"), None)
    return jax.shard_map(
        shards,
        mesh=mesh,
        in_specs=(rows, rows, rows, rows, P("grp", None)),
        out_specs=(rows, rows, rows, rows),
        check_vma=False,
    )
```

```python
import functools
import math

import jax
import jax.numpy as jnp
from jax import lax
from jax.experimental import pallas as pl
from jax.experimental.pallas import tpu as pltpu
from jax.sharding import PartitionSpec as P

HEAD_DIM = 64
NEVER = -1e30
SCORE_SCALE = HEAD_DIM**-0.5 / math.log(2)
LOW = jnp.bfloat16
VMEM = pl.BlockSpec(memory_space=pltpu.VMEM)
SMEM = pl.BlockSpec(memory_space=pltpu.SMEM)


def dot(left, right):
    return jnp.dot(left, right, preferred_element_type=jnp.float32)


def call(kernel, name, outs, *args, limit=8, scratch=(), cost=None, specs=None):
    return pl.pallas_call(
        kernel,
        out_shape=outs,
        in_specs=specs or [VMEM] * len(args),
        out_specs=[VMEM] * len(outs),
        scratch_shapes=scratch,
        name=name,
        cost_estimate=cost,
        compiler_params=pltpu.CompilerParams(vmem_limit_bytes=limit * 1024 * 1024),
    )(*args)


def partners(node):
    turn = 1 - 2 * (node % 2)
    return node + turn, node - turn


def pair_routes(owners, heads):
    routes = []
    for step in range(2):
        route = []
        for n in range(owners):
            other = partners(n)[step]
            for h in range(heads):
                target = other * heads + h if 0 <= other < owners else n * heads + (h ^ 1)
                route.append((n * heads + h, target))
        routes.append(route)
    return routes


def prep_kernel(heads, owners, local_count, per_patch, rows, nbr_ref, after_ref, bias_ref, slot_ref):
    me, node = lax.axis_index("head"), lax.axis_index("node")
    pair = partners(node)
    queries = heads * rows
    own = [[jnp.int32(p == k) for k in range(local_count)] for p in range(local_count)]
    out_of = [[jnp.int32(0), jnp.int32(0)] for _ in range(local_count)]
    for p in range(local_count):
        for j in range(nbr_ref.shape[1]):
            entry = nbr_ref[node * local_count + p, j]
            for k in range(local_count):
                own[p][k] += jnp.where(entry == node * local_count + k, 1, 0)
            for s in range(2):
                start = pair[s] * local_count
                inside = jnp.logical_and(entry >= start, entry < start + local_count)
                out_of[p][s] += jnp.where(inside, 1, 0)

    def choose(index, values):
        value = values[0]
        for i in range(1, len(values)):
            value = jnp.where(index == i, values[i], value)
        return value

    patch_of = [(me ^ d) // per_patch for d in range(heads)]
    counts = [
        [choose(patch_of[e], [choose(patch_of[d], own[p]) for p in range(local_count)]) for e in range(heads)]
        for d in range(heads)
    ]
    for s in range(2):
        counts.append([choose(patch_of[e], [out_of[p][s] for p in range(local_count)]) for e in range(heads)])
    lane_block = lax.broadcasted_iota(jnp.int32, (1, queries), 1) // rows
    for b, row_counts in enumerate(counts):
        row = jnp.zeros((1, queries), jnp.float32)
        for e in range(heads):
            row = jnp.where(lane_block == e, row_counts[e].astype(jnp.float32), row)
        row = jnp.where(row > 0.5, jnp.log(jnp.maximum(row, 1.0)) * (1 / math.log(2)), NEVER)
        bias_ref[b : b + 1, :] = row
    for s in range(2):
        inside = jnp.logical_and(pair[s] >= 0, pair[s] < owners)
        first = jnp.where(inside, pair[s], 0) * local_count
        chosen = jnp.int32(0)
        for p in range(local_count):
            for j in range(nbr_ref.shape[1]):
                entry = nbr_ref[first + p, j] - node * local_count
                mine = jnp.logical_and(entry >= 0, entry < local_count)
                chosen = jnp.where(jnp.logical_and(inside, mine), entry, chosen)
        for t in range(per_patch):
            slot = me ^ (chosen * per_patch + t)
            slot_ref[s * per_patch + t : s * per_patch + t + 1, :] = jnp.full((1, slot_ref.shape[1]), slot)


def pack_kernel(heads, one, two, *refs):
    me = lax.axis_index("head")
    width = refs[-1].shape[-1]
    for d, out in enumerate(refs[-heads:]):
        cols = pl.ds(pl.multiple_of((me ^ d) * width, width), width)
        out[0, 0], out[0, 1] = one[:, cols], two[:, cols]


def pick_kernel(heads, places, slot_ref, *refs):
    arrays, outs = refs[:-2], refs[-2:]
    rows = arrays[0].shape[2]
    per_patch = outs[0].shape[1] // rows
    blocks = [arrays[a][j] for a, j in places]
    for s, out in enumerate(outs):
        for t in range(per_patch):
            slot = slot_ref[s * per_patch + t : s * per_patch + t + 1, :]
            value = blocks[0]
            for d in range(1, heads):
                value = jnp.where(jnp.broadcast_to(slot == d, value.shape[1:])[None], blocks[d], value)
            out[:, t * rows : (t + 1) * rows, :] = value


def spread(bias_ref, first, sizes):
    queries = bias_ref.shape[1]
    rows = [jnp.broadcast_to(bias_ref[first + i : first + i + 1, :], (n, queries)) for i, n in enumerate(sizes)]
    return jnp.concatenate(rows, 0)


def joined(arrays, places, which):
    return jnp.concatenate([arrays[a][j, which] for a, j in places], 0)


def near_kernel(heads, places, count, bias_ref, *refs):
    kv, qg, outs = refs[:count], refs[count : 2 * count], refs[2 * count :]
    exps_ref, gw_ref, stat_ref, *sides = outs
    rows, width = kv[0].shape[2:]
    queries = heads * rows
    groups = width // HEAD_DIM
    bias = spread(bias_ref, 0, [rows] * heads)
    keys, values = joined(kv, places, 0), joined(kv, places, 1)
    lane_head = lax.broadcasted_iota(jnp.int32, (1, width), 1) // HEAD_DIM
    for which, (down, across) in enumerate((sides[:2], sides[2:])):
        whole = joined(qg, places, which)
        turned = whole.T
        across[...] = jnp.zeros_like(across)
        for head in range(groups):
            feats = slice(head * HEAD_DIM, (head + 1) * HEAD_DIM)
            lanes = slice(head * queries, (head + 1) * queries)
            down[lanes, :] = jnp.where(lane_head == head, whole, jnp.zeros_like(whole))
            across[feats, lanes] = turned[feats]
    for head in range(groups):
        lanes = slice(head * queries, (head + 1) * queries)
        scores = dot(keys, sides[1][:, lanes]) * SCORE_SCALE + bias
        top = jnp.max(scores, 0, keepdims=True)
        exps = jnp.exp2(scores - top)
        grad_weights = dot(values, sides[3][:, lanes])
        exps_ref[:, lanes] = exps
        gw_ref[:, lanes] = grad_weights
        stat_ref[0:1, lanes] = top
        stat_ref[1:2, lanes] = jnp.sum(exps, 0, keepdims=True)
        stat_ref[2:3, lanes] = jnp.sum(exps * grad_weights, 0, keepdims=True)


def first_kernel(heads, bias_ref, query_across, grad_across, keys_ref, exps_ref, gw_ref, stat_ref):
    queries = bias_ref.shape[1]
    patch, width = keys_ref.shape[1:]
    bias = spread(bias_ref, heads, [patch])
    for head in range(width // HEAD_DIM):
        lanes = slice(head * queries, (head + 1) * queries)
        scores = dot(keys_ref[0], query_across[:, lanes]) * SCORE_SCALE + bias
        top = jnp.max(scores, 0, keepdims=True)
        exps = jnp.where(bias > NEVER, jnp.exp2(scores - top), 0.0)
        grad_weights = dot(keys_ref[1], grad_across[:, lanes])
        exps_ref[:, lanes] = exps
        gw_ref[:, lanes] = grad_weights
        stat_ref[0:1, lanes] = top
        stat_ref[1:2, lanes] = jnp.sum(exps, 0, keepdims=True)
        stat_ref[2:3, lanes] = jnp.sum(exps * grad_weights, 0, keepdims=True)


def far_kernel(
    heads, owners, places, bias_ref, stat_ref, exps_ref, gw_ref, first_ref, query_down, query_across, grad_down, *refs
):
    grad_across, near_exps_ref, near_gw_ref = refs[:3]
    kv, slabs = refs[3 : heads + 3], refs[heads + 3 : heads + 5]
    w_ref, ds_ref, final_ref, far_a, far_b, *early, near_out, own_w_ref, own_ds_ref = refs[heads + 5 :]
    second_ref = slabs[1]
    patch, width = second_ref.shape[1:]
    queries = bias_ref.shape[1]
    node = lax.axis_index("node")
    other = partners(node)[1]
    both = jnp.logical_and(other >= 0, other < owners)

    def softmax(second):
        bias = spread(bias_ref, heads + 1, [patch]) if second else None
        for head in range(width // HEAD_DIM):
            lanes = slice(head * queries, (head + 1) * queries)
            near_top, first_top = stat_ref[0:1, lanes], first_ref[0:1, lanes]
            top = jnp.maximum(near_top, first_top)
            if second:
                scores = dot(second_ref[0], query_across[:, lanes]) * SCORE_SCALE + bias
                top = jnp.maximum(top, jnp.max(scores, 0, keepdims=True))
                exps = jnp.exp2(scores - top)
                grad_weights = dot(second_ref[1], grad_across[:, lanes])
            shrink, first_shrink = jnp.exp2(near_top - top), jnp.exp2(first_top - top)
            total = shrink * stat_ref[1:2, lanes] + first_shrink * first_ref[1:2, lanes]
            if second:
                total = total + jnp.sum(exps, 0, keepdims=True)
            part = 1.0 / total
            shrink, first_shrink = shrink * part, first_shrink * part
            row_dots = shrink * stat_ref[2:3, lanes] + first_shrink * first_ref[2:3, lanes]
            if second:
                weights = exps * part
                row_dots = row_dots + jnp.sum(weights * grad_weights, 0, keepdims=True)
                w_ref[patch:, lanes] = weights.astype(LOW)
                ds_ref[patch:, lanes] = (weights * (grad_weights - row_dots)).astype(LOW)
            weights = exps_ref[:, lanes] * first_shrink
            w_ref[:patch, lanes] = weights.astype(LOW)
            ds_ref[:patch, lanes] = (weights * (gw_ref[:, lanes] - row_dots)).astype(LOW)
            final_ref[0:1, lanes] = shrink
            final_ref[1:2, lanes] = row_dots

    @pl.when(both)
    def _():
        softmax(True)
        key_grad = dot(ds_ref[...], query_down[...]) * HEAD_DIM**-0.5
        value_grad = dot(w_ref[...], grad_down[...])
        for s, out in enumerate((far_a, far_b)):
            span = slice(s * patch, (s + 1) * patch)
            out[0], out[1] = key_grad[span].astype(LOW), value_grad[span].astype(LOW)

    @pl.when(jnp.logical_not(both))
    def _():
        softmax(False)
        far_a[0] = (dot(ds_ref[:patch, :], query_down[...]) * HEAD_DIM**-0.5).astype(LOW)
        far_a[1] = dot(w_ref[:patch, :], grad_down[...]).astype(LOW)
        far_b[...] = jnp.zeros_like(far_b)
        w_ref[patch:, :] = jnp.zeros((patch, w_ref.shape[1]), LOW)
        ds_ref[patch:, :] = jnp.zeros((patch, ds_ref.shape[1]), LOW)

    @pl.when(node == 0)
    def _():
        weights_of = final_ref, near_exps_ref, near_gw_ref, w_ref, ds_ref
        rest(places, weights_of, (query_down, grad_down), kv, slabs, early, near_out, own_w_ref, own_ds_ref)


def rest(places, weights_of, downs, kv, far, outs, near_out, w_ref, ds_ref):
    heads = len(places)
    final_ref, exps_ref, gw_ref, far_w_ref, far_ds_ref = weights_of
    query_down, grad_down = downs
    rows, width = kv[0].shape[2:]
    queries = heads * rows
    keys_t, values_t = joined(kv, places, 0).T, joined(kv, places, 1).T
    far_keys_t = jnp.concatenate([r[0] for r in far], 0).T
    far_values_t = jnp.concatenate([r[1] for r in far], 0).T
    mixed_t, qgrad_t = [], []
    for head in range(width // HEAD_DIM):
        feats = slice(head * HEAD_DIM, (head + 1) * HEAD_DIM)
        lanes = slice(head * queries, (head + 1) * queries)
        weights = exps_ref[:, lanes] * final_ref[0:1, lanes]
        low = weights.astype(LOW)
        grad_scores = (weights * (gw_ref[:, lanes] - final_ref[1:2, lanes])).astype(LOW)
        w_ref[:, lanes] = low
        ds_ref[:, lanes] = grad_scores
        mixed_t.append(dot(values_t[feats], low) + dot(far_values_t[feats], far_w_ref[:, lanes]))
        qgrad_t.append((dot(keys_t[feats], grad_scores) + dot(far_keys_t[feats], far_ds_ref[:, lanes])) * HEAD_DIM**-0.5)
    mixed = jnp.concatenate(mixed_t, 0).T.astype(LOW)
    qgrad = jnp.concatenate(qgrad_t, 0).T.astype(LOW)
    key_grad = dot(ds_ref[...], query_down[...]) * HEAD_DIM**-0.5
    value_grad = dot(w_ref[...], grad_down[...])
    for d, out in enumerate(outs):
        span = slice(d * rows, (d + 1) * rows)
        out[0, 0], out[0, 1] = mixed[span], qgrad[span]
        near_out[d, 0], near_out[d, 1] = key_grad[span].astype(LOW), value_grad[span].astype(LOW)


def rest_kernel(heads, places, final_ref, exps_ref, gw_ref, far_w_ref, far_ds_ref, query_down, grad_down, *refs):
    kv, far, early = refs[:heads], refs[heads : heads + 2], refs[heads + 2 : 2 * heads + 3]
    *outs, near_out, w_ref, ds_ref = refs[2 * heads + 3 :]
    first = lax.axis_index("node") == 0

    @pl.when(first)
    def _():
        for ref, out in zip(early, outs + [near_out]):
            out[...] = ref[...]

    @pl.when(jnp.logical_not(first))
    def _():
        weights_of = final_ref, exps_ref, gw_ref, far_w_ref, far_ds_ref
        rest(places, weights_of, (query_down, grad_down), kv, far, outs, near_out, w_ref, ds_ref)


def merge_kernel(heads, slot_ref, near, back_a, back_b, *outs):
    rows = near.shape[2]
    per_patch = back_a.shape[1] // rows
    me = lax.axis_index("head")
    for d in range(heads):
        total = near[d].astype(jnp.float32)
        part = lax.rem(me ^ d, per_patch)
        for s, back in enumerate((back_a, back_b)):
            slot = slot_ref[pl.ds(s * per_patch + part, 1), :]
            term = back[:, pl.ds(pl.multiple_of(part * rows, rows), rows), :].astype(jnp.float32)
            total = total + jnp.where((slot == d)[None], term, 0.0)
        outs[d][0] = total.astype(LOW)


def join_kernel(*refs):
    count = len(refs) // 3
    for i, out in enumerate(refs[2 * count :]):
        out[0, 0], out[0, 1] = refs[2 * i][...], refs[2 * i + 1][...]


def unpack_kernel(heads, places, *refs):
    arrays, outs = refs[:-2], refs[-2:]
    width = arrays[0].shape[-1]
    me = lax.axis_index("head")
    for d, (a, j) in enumerate(places):
        cols = pl.ds(pl.multiple_of((me ^ d) * width, width), width)
        outs[0][:, cols], outs[1][:, cols] = arrays[a][j, 0], arrays[a][j, 1]


def far_first(heads):
    return [0] + sorted(range(1, heads), key=lambda d: (-(d >> 1), d))


def exchange(blocks, order):
    heads = len(blocks)
    swaps = [[(i, i ^ d) for i in range(heads)] for d in range(heads)]
    return [lax.ppermute(blocks[d], "head", swaps[d]) if d else blocks[0] for d in order]


def cut(one, two, heads):
    me = lax.axis_index("head")
    width = one.shape[1] // heads
    starts = [(me ^ d) * width for d in range(heads)]
    parts = [[lax.dynamic_slice_in_dim(a, at, width, 1) for a in (one, two)] for at in starts]
    return call(join_kernel, "join", [jax.ShapeDtypeStruct((1, 2) + parts[0][0].shape, LOW)] * heads, *sum(parts, []))


def shards(queries, key_rows, value_rows, out_grads, neighbours):
    rows, features = queries.shape
    heads, owners = lax.axis_size("head"), lax.axis_size("node")
    width = features // heads
    local_count = neighbours.shape[0] // owners
    per_patch = heads // local_count
    patch = rows * per_patch
    block = jax.ShapeDtypeStruct((1, 2, rows, width), LOW)
    order, downward = far_first(heads), [0] + list(range(heads - 1, 0, -1))
    places = [(order.index(d), 0) for d in range(heads)]
    near_shape = jax.ShapeDtypeStruct((heads, 2, rows, width), LOW)
    slab = jax.ShapeDtypeStruct((2, patch, width), LOW)
    whole = jax.ShapeDtypeStruct((rows, features), LOW)
    routes = pair_routes(owners, heads)

    kv = exchange(cut(key_rows, value_rows, heads), order)
    bias, slots = call(
        functools.partial(prep_kernel, heads, owners, local_count, per_patch, rows),
        "prep",
        [
            jax.ShapeDtypeStruct((heads + 2, heads * rows), jnp.float32),
            jax.ShapeDtypeStruct((2 * per_patch, width), jnp.int32),
        ],
        neighbours,
        kv[0],
        specs=[SMEM, VMEM],
    )
    pack = functools.partial(pack_kernel, heads)
    qg = exchange(call(pack, "pack", [block] * heads, queries, out_grads, slots), order)
    picked = call(functools.partial(pick_kernel, heads, places), "pick", [slab] * 2, slots, *kv)
    far = [lax.ppermute(p, ("node", "head"), r) for p, r in zip(picked, routes)]
    lanes = width // HEAD_DIM * heads * rows
    own, other = heads * rows, 2 * patch
    work = pl.CostEstimate(flops=1500000000, bytes_accessed=1, transcendentals=0)

    def table(height, kind=jnp.float32):
        return jax.ShapeDtypeStruct((height, lanes), kind)

    down = jax.ShapeDtypeStruct((lanes, width), LOW)
    across = jax.ShapeDtypeStruct((width, lanes), LOW)
    exps, grad_weights, stats, *sides = call(
        functools.partial(near_kernel, heads, places, len(kv)),
        "near",
        [table(own), table(own), table(3), down, across, down, across],
        bias,
        *kv,
        *qg,
        cost=work,
    )
    first = call(
        functools.partial(first_kernel, heads),
        "first",
        [table(patch), table(patch), table(3)],
        bias,
        sides[1],
        sides[3],
        far[0],
    )
    far_w, far_ds, final, far_a, far_b, *early = call(
        functools.partial(far_kernel, heads, owners, places),
        "far",
        [table(other, LOW), table(other, LOW), table(2), slab, slab] + [block] * heads + [near_shape],
        bias,
        stats,
        *first,
        *sides,
        exps,
        grad_weights,
        *kv,
        *far,
        scratch=[pltpu.VMEM((own, lanes), LOW)] * 2,
        limit=12,
        cost=work,
    )
    *mq, near = call(
        functools.partial(rest_kernel, heads, places),
        "rest",
        [block] * heads + [near_shape],
        final,
        exps,
        grad_weights,
        far_w,
        far_ds,
        sides[0],
        sides[2],
        *kv,
        *far,
        *early,
        scratch=[pltpu.VMEM((own, lanes), LOW)] * 2,
        cost=work,
    )
    back = [lax.ppermute(p, ("node", "head"), r) for p, r in zip((far_a, far_b), routes)]
    mq = exchange(mq, downward)
    merged = call(functools.partial(merge_kernel, heads), "merge", [block] * heads, slots, near, *back)
    kv_grads = exchange(merged, order)
    unpack = functools.partial(unpack_kernel, heads)
    mq_places = [(downward.index(d), 0) for d in range(heads)]
    mixed, query_grad = call(functools.partial(unpack, mq_places), "unpack", [whole] * 2, *mq)
    key_grad, value_grad = call(functools.partial(unpack, places), "unpack", [whole] * 2, *kv_grads)
    return mixed, query_grad, key_grad, value_grad


def solution(mesh):
    rows = P(("grp", "node", "head"), None)
    return jax.shard_map(
        shards,
        mesh=mesh,
        in_specs=(rows, rows, rows, rows, P("grp", None)),
        out_specs=(rows, rows, rows, rows),
        check_vma=False,
    )
```
